512 devices in a mesh: ax: 64 (over x, y_lo, z), az: 8 (over y_hi, core).
Axes of the slice: x: 4, y: 8 (y_hi: 4, y_lo: 2; y = y_hi * 2 + y_lo), z: 8, core: 2. Of those that a mesh axis runs over, the one named last changes fastest.
Arguments:
- layer_input: bfloat16 [64, 128, 128, 128], P(None, 'ax', 'az'), may hold values from -6 to 6
- pre_act: bfloat16 [64, 128, 128, 128], P(None, 'ax', 'az'), may hold values from -6 to 6
- out_grad: bfloat16 [64, 128, 128, 128], P(None, 'ax', 'az'), may hold values from -6 to 6
- point_weight: bfloat16 [64, 64], replicated, may hold values from -0.75 to 0.75
- spec_weight: bfloat16 [512, 32, 4096], P(('az', 'ax')), may hold values from -0.75 to 0.75
- saved_coeffs: bfloat16 [512, 2048], P(('az', 'ax')), may hold values from -0.625 to 0.625
Outputs:
- input_grad: bfloat16 [64, 128, 128, 128], P(None, 'ax', 'az')
- point_grad: float32 [64, 64], replicated
- bias_grad: float32 [64], replicated
- spec_grad: bfloat16 [512, 32, 4096], P(('az', 'ax'))
The draws below stay inside these ranges and needn't reach their ends.
All inputs are finite; a program needn't handle non-finite values.
Results may differ from the reference program's by a relative error of at most 0.012.
Values may be sent and summed in bfloat16 or wider, within the bound.
No kernel may reach another device: no remote copies, remote signals or barrier semaphores. Data moves between devices by JAX's collectives and lax.ppermute only.
A program may use at most 64 MiB of HBM per device.

```python
import math
import jax
import jax.numpy as jnp
from jax import lax

CH = 64
MX = 32
MT = 16
MR = 16
NR = 128
NX = 128
NT = 128
NPAIR = 512
NCELLS = 2097152


def block_scale(own_key, shape, shards, smallest, high):
    gain, own = 1.0, jax.random.fold_in(own_key, 6)
    for axis_at, parts in shards:
        steps = jnp.exp(jax.random.uniform(jax.random.fold_in(own, axis_at), (parts,), jnp.float32, smallest / len(shards), high / len(shards)))
        gain = gain * jnp.repeat(steps, shape[axis_at] // parts).reshape([-1 if axis == axis_at else 1 for axis in range(len(shape))])
    return gain


def bell_draw(stream_key, shape, width, reach, pieces=(), dtype=jnp.bfloat16):
    level = block_scale(stream_key, shape, pieces, -0.22, 0.18) if pieces else 1.0
    result = jax.random.normal(stream_key, shape, jnp.float32) * width * level
    return jnp.minimum(jnp.maximum(result, -reach), reach).astype(dtype)


def setup_inputs(seed: int = 0) -> dict:
    streams_of = jax.random.split(jax.random.key(seed), 7)
    layer_input = bell_draw(streams_of[0], (CH, NX, NT, NR), 1.0, 6.0, ((1, 64), (2, 8)))
    pre_act = bell_draw(streams_of[1], (CH, NX, NT, NR), 1.0, 6.0, ((1, 64), (2, 8)))
    out_grad = bell_draw(streams_of[2], (CH, NX, NT, NR), 1.0, 6.0, ((1, 64), (2, 8)))
    point_weight = bell_draw(streams_of[3], (CH, CH), CH ** -0.5, 0.75)
    spec_weight = bell_draw(streams_of[4], (NPAIR, MX, CH * CH), CH ** -0.5, 0.75, ((0, 512),))
    saved_coeffs = bell_draw(streams_of[5], (NPAIR, MX * CH), 0.1, 0.625, ((0, 512),))
    return {"layer_input": layer_input, "pre_act": pre_act, "out_grad": out_grad, "point_weight": point_weight, "spec_weight": spec_weight, "saved_coeffs": saved_coeffs}


def gelu_slope(values):
    density = jnp.exp(-0.5 * values * values) * (1.0 / math.sqrt(2.0 * math.pi))
    return 0.5 * (1.0 + lax.erf(values * (1.0 / math.sqrt(2.0)))) + values * density

def cosine_table(extent, wanted, offset, height):
    places = (offset + jnp.arange(height)).astype(jnp.float32) + 0.5
    orders = jnp.arange(wanted).astype(jnp.float32)
    scaled = math.sqrt(2.0 / extent) * jnp.cos(math.pi * places[:, None] * orders[None, :] / extent)
    scaled = jnp.where(orders[None, :] == 0.0, scaled * (1.0 / math.sqrt(2.0)), scaled)
    return scaled.astype(jnp.bfloat16)

def cycle_table(extent, half_modes, offset, height):
    places = (offset + jnp.arange(height)).astype(jnp.float32) + 0.5
    angles = 2.0 * math.pi * places / extent
    orders = jnp.arange(half_modes).astype(jnp.float32)
    cosines = math.sqrt(2.0 / extent) * jnp.cos(angles[:, None] * orders[None, :])
    cosines = jnp.where(orders[None, :] == 0.0, cosines * (1.0 / math.sqrt(2.0)), cosines)
    sine_part = math.sqrt(2.0 / extent) * jnp.sin(angles[:, None] * (orders[None, :] + 1.0))
    return jnp.concatenate([cosines, sine_part], axis=1).astype(jnp.bfloat16)

def reference(layer_input, pre_act, out_grad, point_weight, spec_weight, saved_coeffs):
    radial_table = cosine_table(NR, MR, 0, NR)
    radial_wide = radial_table.astype(jnp.float32)
    cycle_wide = cycle_table(NT, MT, 0, NT).astype(jnp.float32)
    axial_wide = cosine_table(NX, MX, 0, NX).astype(jnp.float32)
    synth_gain = math.sqrt(NX * NT * NR / (2.0 * MX * MT * MR))
    norm_scale = 1.0 / math.sqrt(NCELLS)
    inputs_moved = jnp.moveaxis(layer_input, 1, 0)
    pre_moved = jnp.moveaxis(pre_act, 1, 0)
    grads_moved = jnp.moveaxis(out_grad, 1, 0)

    def forward_slice(slices):
        input_slab, pre_slab, grad_slab = slices
        grad_pre = (grad_slab.astype(jnp.float32) * gelu_slope(pre_slab.astype(jnp.float32))).astype(jnp.bfloat16)
        point_term = jnp.dot(input_slab.reshape(CH, NT * NR), grad_pre.reshape(CH, NT * NR).T, preferred_element_type=jnp.float32)
        bias_term = lax.optimization_barrier(jnp.sum(grad_pre.astype(jnp.float32), axis=(1, 2)))
        radial_coef = jnp.dot(grad_pre.reshape(CH * NT, NR), radial_table, preferred_element_type=jnp.float32).reshape(CH, NT, MR)
        cycle_coef = jnp.einsum('ctk,tm->mkc', radial_coef, cycle_wide, precision=lax.Precision.HIGHEST)
        return (point_term, bias_term, cycle_coef.astype(jnp.bfloat16).reshape(NPAIR, CH))
    point_terms, bias_terms, spectral_in = lax.map(forward_slice, (inputs_moved, pre_moved, grads_moved))
    point_grad = lax.optimization_barrier(jnp.sum(point_terms, axis=0)) * norm_scale
    bias_grad = lax.optimization_barrier(jnp.sum(bias_terms, axis=0)) * norm_scale
    axial_sum = jnp.einsum('xpc,xk->pkc', spectral_in.astype(jnp.float32), axial_wide, precision=lax.Precision.HIGHEST)
    mode_grad = (synth_gain * axial_sum).astype(jnp.bfloat16)
    mixing = spec_weight.reshape(NPAIR, MX, CH, CH).astype(jnp.float32)
    coef_grad = jnp.einsum('pkio,pko->pki', mixing, mode_grad.astype(jnp.float32), precision=lax.Precision.HIGHEST).astype(jnp.bfloat16)
    saved_modes = saved_coeffs.reshape(NPAIR, MX, CH).astype(jnp.float32)
    spec_grad = (saved_modes[:, :, :, None] * mode_grad.astype(jnp.float32)[:, :, None, :]).astype(jnp.bfloat16).reshape(NPAIR, MX, CH * CH)
    slab_modes = jnp.einsum('pki,xk->xpi', coef_grad.astype(jnp.float32), axial_wide, precision=lax.Precision.HIGHEST).astype(jnp.bfloat16)

    def backward_slice(slices):
        mode_slab, pre_slab, grad_slab = slices
        grad_pre = (grad_slab.astype(jnp.float32) * gelu_slope(pre_slab.astype(jnp.float32))).astype(jnp.bfloat16)
        cycle_part = jnp.einsum('mkc,tm->ctk', mode_slab.reshape(2 * MT, MR, CH).astype(jnp.float32), cycle_wide, precision=lax.Precision.HIGHEST)
        spectral_part = jnp.einsum('ctk,rk->ctr', cycle_part, radial_wide, precision=lax.Precision.HIGHEST)
        point_part = jnp.dot(point_weight, grad_pre.reshape(CH, NT * NR), preferred_element_type=jnp.float32).reshape(CH, NT, NR)
        return (spectral_part + point_part).astype(jnp.bfloat16)
    input_moved = lax.map(backward_slice, (slab_modes, pre_moved, grads_moved))
    input_grad = jnp.moveaxis(input_moved, 0, 1)
    return (input_grad, point_grad, bias_grad, spec_grad)
```

```python
import math

import jax
import jax.numpy as jnp
from jax import lax
from jax.sharding import PartitionSpec as P

CH = 64
MX = 32
MT = 16
MR = 16


def gelu_slope(values):
    density = jnp.exp(-0.5 * values * values) * (1.0 / math.sqrt(2.0 * math.pi))
    return 0.5 * (1.0 + lax.erf(values * (1.0 / math.sqrt(2.0)))) + values * density


def cosine_table(extent, wanted, offset, height):
    places = (offset + jnp.arange(height)).astype(jnp.float32) + 0.5
    orders = jnp.arange(wanted).astype(jnp.float32)
    scaled = math.sqrt(2.0 / extent) * jnp.cos(math.pi * places[:, None] * orders[None, :] / extent)
    scaled = jnp.where(orders[None, :] == 0.0, scaled * (1.0 / math.sqrt(2.0)), scaled)
    return scaled.astype(jnp.bfloat16)


def cycle_table(extent, half_modes, offset, height):
    places = (offset + jnp.arange(height)).astype(jnp.float32) + 0.5
    angles = 2.0 * math.pi * places / extent
    orders = jnp.arange(half_modes).astype(jnp.float32)
    cosines = math.sqrt(2.0 / extent) * jnp.cos(angles[:, None] * orders[None, :])
    cosines = jnp.where(orders[None, :] == 0.0, cosines * (1.0 / math.sqrt(2.0)), cosines)
    sine_part = math.sqrt(2.0 / extent) * jnp.sin(angles[:, None] * (orders[None, :] + 1.0))
    return jnp.concatenate([cosines, sine_part], axis=1).astype(jnp.bfloat16)


def two_parts(values):
    high = lax.reduce_precision(values, 8, 7)
    return high.astype(jnp.bfloat16), (values - high).astype(jnp.bfloat16)


def per_device(layer_input, pre_act, out_grad, point_weight, spec_weight, saved_coeffs):
    axial_devices = lax.axis_size("ax")
    cycle_devices = lax.axis_size("az")
    devices = axial_devices * cycle_devices
    slab_length = layer_input.shape[1]
    sector_length = layer_input.shape[2]
    radial_length = layer_input.shape[3]
    axial_total = slab_length * axial_devices
    cycle_total = sector_length * cycle_devices
    cells_total = axial_total * cycle_total * radial_length
    synth_gain = math.sqrt(cells_total / (2.0 * MX * MT * MR))
    norm_scale = 1.0 / math.sqrt(cells_total)
    row = slab_length * CH
    sums_total = CH * CH + CH
    share = -(-sums_total // devices)
    radial_table = cosine_table(radial_length, MR, 0, radial_length)
    axial_table = cosine_table(axial_total, MX, 0, axial_total)
    cycle_local = cycle_table(cycle_total, MT, lax.axis_index("az") * sector_length, sector_length)

    grad_pre = (out_grad.astype(jnp.float32) * gelu_slope(pre_act.astype(jnp.float32))).astype(jnp.bfloat16)
    point_local = jnp.einsum("ixtr,oxtr->io", layer_input, grad_pre, preferred_element_type=jnp.float32)
    bias_local = jnp.sum(grad_pre.astype(jnp.float32), axis=(1, 2, 3))
    radial_coef = jnp.einsum(
        "ixtr,rk->ixtk", grad_pre, radial_table, preferred_element_type=jnp.float32
    ).astype(jnp.bfloat16)
    modes = jnp.einsum("ixtk,tm->mkxi", radial_coef, cycle_local, preferred_element_type=jnp.float32)
    modes = modes.astype(jnp.bfloat16).reshape(devices, row)
    sums = jnp.concatenate([point_local.reshape(-1), bias_local, jnp.zeros(share * devices - sums_total, jnp.float32)])
    high, low = two_parts(sums.reshape(devices, share))
    sums_row = jnp.pad(jnp.concatenate([high, low], axis=1), ((0, 0), (0, row - 2 * share)))
    sent = jnp.stack([modes, sums_row], axis=1)
    got = lax.all_to_all(sent, ("az", "ax"), 0, 0, tiled=True)

    spectral_in = jnp.sum(
        got[:, 0].reshape(cycle_devices, axial_total, CH).astype(jnp.float32), axis=0
    ).astype(jnp.bfloat16)
    sums_here = jnp.sum(got[:, 1, : 2 * share].astype(jnp.float32), axis=0)
    sums_here = (sums_here[:share] + sums_here[share:]) * norm_scale
    mode_grad = synth_gain * jnp.einsum(
        "xi,xk->ki", spectral_in, axial_table, preferred_element_type=jnp.float32
    )
    mode_grad = mode_grad.astype(jnp.bfloat16)
    mixing = spec_weight.reshape(MX, CH, CH)
    coef_grad = jnp.einsum("kio,ko->ki", mixing, mode_grad, preferred_element_type=jnp.float32).astype(jnp.bfloat16)
    saved_modes = saved_coeffs.reshape(MX, CH).astype(jnp.float32)
    spec_grad = (
        (saved_modes[:, :, None] * mode_grad.astype(jnp.float32)[:, None, :])
        .astype(jnp.bfloat16)
        .reshape(1, MX, CH * CH)
    )
    slab_modes = jnp.einsum("ki,xk->xi", coef_grad, axial_table, preferred_element_type=jnp.float32)
    slab_modes = slab_modes.astype(jnp.bfloat16).reshape(1, axial_devices, row)
    slab_modes = jnp.broadcast_to(slab_modes, (cycle_devices, axial_devices, row)).reshape(devices, row)
    high, low = two_parts(sums_here)
    sums_row = jnp.pad(jnp.concatenate([high, low]), (0, row - 2 * share))
    sent = jnp.stack([slab_modes, jnp.broadcast_to(sums_row, (devices, row))], axis=1)
    got = lax.all_to_all(sent, ("az", "ax"), 0, 0, tiled=True)

    cycle_modes = got[:, 0].reshape(2 * MT, MR, slab_length, CH)
    sums_all = got[:, 1, :share].astype(jnp.float32) + got[:, 1, share : 2 * share].astype(jnp.float32)
    sums_all = sums_all.reshape(-1)
    point_grad = sums_all[: CH * CH].reshape(CH, CH)
    bias_grad = sums_all[CH * CH : sums_total]
    point_part = jnp.einsum("io,oxtr->ixtr", point_weight, grad_pre, preferred_element_type=jnp.float32)
    radial_modes = jnp.einsum(
        "mkxi,tm->ixtk", cycle_modes, cycle_local, preferred_element_type=jnp.float32
    ).astype(jnp.bfloat16)
    spectral_part = jnp.einsum("ixtk,rk->ixtr", radial_modes, radial_table, preferred_element_type=jnp.float32)
    input_grad = (spectral_part + point_part).astype(jnp.bfloat16)
    return (input_grad, point_grad, bias_grad, spec_grad)


def solution(mesh):
    return jax.shard_map(
        per_device,
        mesh=mesh,
        in_specs=(
            P(None, "ax", "az", None),
            P(None, "ax", "az", None),
            P(None, "ax", "az", None),
            P(),
            P(("az", "ax"), None, None),
            P(("az", "ax"), None),
        ),
        out_specs=(P(None, "ax", "az", None), P(), P(), P(("az", "ax"), None, None)),
        check_vma=False,
    )
```

```python
import functools
import math

import jax
import jax.numpy as jnp
import numpy as np
from jax import lax
from jax.experimental import pallas as pl
from jax.experimental.pallas import tpu as pltpu
from jax.sharding import PartitionSpec as P

CH = 64
MX = 32
MT = 16
MR = 16
BF = jnp.bfloat16
F32 = jnp.float32
VMEM_LIMIT = 48 * 1024 * 1024


def cosine_table(extent, wanted):
    places = np.arange(extent) + 0.5
    orders = np.arange(wanted)
    table = math.sqrt(2.0 / extent) * np.cos(math.pi * places[:, None] * orders[None, :] / extent)
    table[:, 0] *= 1.0 / math.sqrt(2.0)
    return table.astype(np.float32).astype(jnp.bfloat16).astype(np.float32)


def cycle_table(extent, half_modes):
    angles = 2.0 * math.pi * (np.arange(extent) + 0.5) / extent
    orders = np.arange(half_modes)
    cosines = math.sqrt(2.0 / extent) * np.cos(angles[:, None] * orders[None, :])
    cosines[:, 0] *= 1.0 / math.sqrt(2.0)
    sines = math.sqrt(2.0 / extent) * np.sin(angles[:, None] * (orders[None, :] + 1.0))
    table = np.concatenate([cosines, sines], axis=1)
    return table.astype(np.float32).astype(jnp.bfloat16).astype(np.float32)


def make_tables(axial, cycle, radial, cycle_devices):
    sector = cycle // cycle_devices
    pairs = 2 * MT * MR
    radial_table, axial_table = cosine_table(radial, MR), cosine_table(axial, MX)
    cycle_all = cycle_table(cycle, MT)
    tables = {}
    swap = np.zeros((16, 16, 16, 16), np.float32)
    for a in range(16):
        for b in range(16):
            swap[a, b, b, a] = 1.0
    tables["swap"] = swap.reshape(256, 256)
    ends = np.zeros((32, radial), np.float32)
    ends[:MR] = radial_table.T
    ends[MR:] = 1.0
    tables["ends"] = ends
    forward = np.zeros((cycle_devices, 2 * MT, MR, 2, sector, MR), np.float32)
    for k in range(MR):
        part = cycle_all.reshape(cycle_devices, sector, 2 * MT)
        forward[:, :, k, 0, :, k] = part.transpose(0, 2, 1)
    forward = forward.reshape(cycle_devices, 2 * pairs, sector * MR)
    tables["forward"] = forward
    tables["inverse"] = forward.transpose(0, 2, 1)
    rows = np.zeros((pairs, 2, 128), np.float32)
    for p in range(pairs):
        rows[p, 1, CH if p % 8 == 7 else p // 8] = 1.0
    tables["place"] = rows.reshape(2 * pairs, 128)
    pick = np.zeros((80, pairs, 2), np.float32)
    for i in range(CH):
        pick[i, 8 * i, 1] = 1.0
    pick[CH, 7, 1] = 1.0
    tables["pick"] = pick.reshape(80, 2 * pairs)
    gather = np.zeros((80, cycle_devices, pairs // cycle_devices, 2), np.float32)
    ax_devices = pairs // cycle_devices
    slab = axial // ax_devices
    by_slab = axial_table.reshape(ax_devices, slab, MX)
    gather[: slab * MX, :, :, 0] = by_slab.transpose(1, 2, 0).reshape(slab * MX, 1, ax_devices)
    gather[slab * MX :, :, :, 1] = 1.0
    tables["gather"] = gather.reshape(80, 2 * pairs)
    spread = np.zeros((ax_devices, 2, slab * MX), np.float32)
    spread[:, 0, :] = by_slab.reshape(ax_devices, slab * MX)
    tables["spread"] = spread.reshape(2 * ax_devices, slab * MX)
    halves = (np.arange(128)[:, None] // 64 == np.arange(128)[None, :] // 64).astype(np.float32)
    tables["halves"] = np.concatenate([halves, halves], axis=0)
    tables["radial"] = np.tile(radial_table.T, (sector, 1))
    tables["same"] = (np.arange(sector * MR)[None, :] // MR == np.arange(sector)[:, None]).astype(np.float32)
    return {name: value.astype(jnp.float32 if name == "same" else jnp.bfloat16) for name, value in tables.items()}


def gelu_slope(values):
    density = jnp.exp(-0.5 * values * values) * (1.0 / math.sqrt(2.0 * math.pi))
    return 0.5 * (1.0 + lax.erf(values * (1.0 / math.sqrt(2.0)))) + values * density


def dot_nn(a, b):
    return lax.dot_general(a, b, (((1,), (0,)), ((), ())), preferred_element_type=F32)


def dot_nt(a, b):
    return lax.dot_general(a, b, (((1,), (1,)), ((), ())), preferred_element_type=F32)


def split_halves(values):
    lane = lax.broadcasted_iota(jnp.int32, values.shape, 1)
    high = values.astype(BF).astype(F32)
    return jnp.where(lane < 64, high, pltpu.roll(values - high, 64, 1))


def first_kernel(steps, where, layer_ref, pre_ref, grad_ref, swap_ref, ends_ref, place_ref, forward_hbm,
                 slope_ref, sent_ref, layer_rows, grad_rows, coefs, forward, sem):
    step = pl.program_id(0)
    copy = pltpu.make_async_copy(forward_hbm.at[where[0]], forward, sem)

    @pl.when(step == 0)
    def _():
        copy.start()

    group = layer_ref.shape[0]
    slope = (grad_ref[...].astype(F32) * gelu_slope(pre_ref[...].astype(F32))).astype(BF)
    slope_ref[...] = slope
    layer = layer_ref[...]
    swap = swap_ref[...]
    for part in range(group // 16):
        for x in range(2):
            rows = pl.ds(pl.multiple_of(x * CH + step * group + part * 16, 16), 16)
            both = jnp.concatenate(
                [layer[part * 16 : part * 16 + 16, x].reshape(256, 128), slope[part * 16 : part * 16 + 16, x].reshape(256, 128)],
                axis=1,
            )
            moved = dot_nn(swap, both).astype(BF)
            layer_rows[:, rows, :] = moved[:, :128].reshape(16, 16, 128)
            grad_rows[:, rows, :] = moved[:, 128:].reshape(16, 16, 128)

    @pl.when(step == steps - 1)
    def _():
        point = jnp.zeros((128, 128), F32)
        bias = jnp.zeros((16, 128), F32)
        for t in range(16):
            left = jnp.concatenate([layer_rows[t], ends_ref[...]], axis=0)
            out = dot_nt(left, grad_rows[t])
            point += out[:128]
            coefs[t * MR : (t + 1) * MR, :] = out[128:144].astype(BF)
            bias += out[144:]
        point = point[:64] + pltpu.roll(point[64:], 64, 1)
        bias = bias + pltpu.roll(bias, 64, 1)
        sums = jnp.concatenate([split_halves(point), split_halves(bias), jnp.zeros((48, 128), F32)], axis=0)
        copy.wait()
        sent = dot_nn(forward[...], coefs[...]) + dot_nn(place_ref[...], sums.astype(BF))
        sent_ref[...] = sent.astype(BF)


def first(layer_input, pre_act, out_grad, tables):
    steps = 4
    group = CH // steps
    field = pl.BlockSpec((group, 2, 16, 128), lambda s, where: (s, 0, 0, 0))

    def whole(shape):
        return pl.BlockSpec(shape, lambda s, where: (0,) * len(shape))

    where = lax.axis_index("az").astype(jnp.int32).reshape(1)
    return pl.pallas_call(
        functools.partial(first_kernel, steps),
        grid_spec=pltpu.PrefetchScalarGridSpec(
            num_scalar_prefetch=1,
            grid=(steps,),
            in_specs=[
                field, field, field, whole((256, 256)), whole((32, 128)), whole((1024, 128)),
                pl.BlockSpec(memory_space=pl.ANY),
            ],
            out_specs=[field, whole((1024, 128))],
            scratch_shapes=[
                pltpu.VMEM((16, 128, 128), BF),
                pltpu.VMEM((16, 128, 128), BF),
                pltpu.VMEM((256, 128), BF),
                pltpu.VMEM((1024, 256), BF),
                pltpu.SemaphoreType.DMA,
            ],
        ),
        out_shape=[
            jax.ShapeDtypeStruct((CH, 2, 16, 128), BF),
            jax.ShapeDtypeStruct((1024, 128), BF),
        ],
        compiler_params=pltpu.CompilerParams(vmem_limit_bytes=60 * 1024 * 1024),
        name="slope_and_modes",
    )(where, layer_input, pre_act, out_grad, tables["swap"], tables["ends"], tables["place"], tables["forward"])


def middle_kernel(gain, norm, got_ref, gather_ref, weight_ref, halves_ref, spread_ref, mode_ref, sent_ref, stack):
    full = dot_nn(gather_ref[...], got_ref[...])
    lane = lax.broadcasted_iota(jnp.int32, (32, 128), 1)
    picked = jnp.where(lane < 64, full[:32], full[32:64])
    mode = (gain * (picked + pltpu.roll(picked, 64, 1))).astype(BF)
    mode_ref[...] = mode
    mode_wide = mode.astype(F32)
    for c in range(32):
        product = weight_ref[0, :, c * 128 : (c + 1) * 128].astype(F32) * mode_wide
        high = product.astype(BF)
        stack[c * 32 : (c + 1) * 32, :128] = high
        stack[c * 32 : (c + 1) * 32, 128:] = (product - high.astype(F32)).astype(BF)
    summed = dot_nn(stack[...], halves_ref[...])
    coef = jnp.zeros((32, 128), F32)
    for c in range(32):
        coef = jnp.where(lane % 64 == c, summed[c * 32 : (c + 1) * 32], coef)
    coef = jnp.concatenate([coef, pltpu.roll(coef, 32, 1)], axis=0).astype(BF)
    slabs = dot_nn(spread_ref[...], coef)
    sums = full[64:80]
    sums = split_halves((sums + pltpu.roll(sums, 64, 1)) * norm)
    row = lax.broadcasted_iota(jnp.int32, (128, 128), 0)
    slabs = jnp.where(row % 2 == 0, slabs, sums[:1]).astype(BF)
    for az in range(8):
        sent_ref[az] = slabs


def middle(got, spec_weight, tables, gain, norm):
    return pl.pallas_call(
        functools.partial(middle_kernel, gain, norm),
        out_shape=[jax.ShapeDtypeStruct((32, 128), BF), jax.ShapeDtypeStruct((8, 128, 128), BF)],
        scratch_shapes=[pltpu.VMEM((1024, 256), BF)],
        compiler_params=pltpu.CompilerParams(vmem_limit_bytes=VMEM_LIMIT),
        name="modes_and_mixing",
    )(got, tables["gather"], spec_weight, tables["halves"], tables["spread"])


def last_kernel(got_ref, pick_ref, radial_ref, same_ref, inverse_ref, point_ref,
                field_ref, weight_ref, bias_ref, columns, wide):
    step = pl.program_id(0)
    group = field_ref.shape[0]

    @pl.when(step == 0)
    def _():
        got = got_ref[...]
        columns[...] = jnp.transpose(dot_nn(inverse_ref[...], got))
        sums = dot_nn(pick_ref[...], got)
        sums = sums + pltpu.roll(sums, 64, 1)
        weight_ref[...] = sums[:64, :64]
        bias_ref[...] = sums[64:72]

    same = same_ref[...]
    for at in range(group):
        for x in range(2):
            place = (at % 2) * 64 + x * 32 + at // 2 + step * (group // 2)
            value = jnp.broadcast_to(columns[pl.ds(place, 1), :], (16, 256)) * same
            wide[(at * 2 + x) * 16 : (at * 2 + x) * 16 + 16, :] = value.astype(BF)
    spectral = dot_nn(wide[...], radial_ref[...])
    field_ref[...] = (spectral.reshape(group, 2, 16, 128) + point_ref[...]).astype(BF)


def last(got, inverse, point_part, tables):
    steps = 4
    group = CH // steps
    field = pl.BlockSpec((group, 2, 16, 128), lambda s: (s, 0, 0, 0))

    def whole(shape):
        return pl.BlockSpec(shape, lambda s: (0,) * len(shape))

    return pl.pallas_call(
        last_kernel,
        grid=(steps,),
        in_specs=[
            whole((1024, 128)), whole((80, 1024)), whole((256, 128)), whole((16, 256)), whole((256, 1024)), field,
        ],
        out_specs=[field, whole((64, 64)), whole((8, 128))],
        scratch_shapes=[pltpu.VMEM((128, 256), F32), pltpu.VMEM((group * 32, 256), BF)],
        out_shape=[
            jax.ShapeDtypeStruct((CH, 2, 16, 128), BF),
            jax.ShapeDtypeStruct((CH, CH), F32),
            jax.ShapeDtypeStruct((8, 128), F32),
        ],
        compiler_params=pltpu.CompilerParams(vmem_limit_bytes=VMEM_LIMIT),
        name="modes_to_field",
    )(got, tables["pick"], tables["radial"], tables["same"], inverse, point_part)


def exchange(rows, devices):
    sent = rows.reshape(devices, 2, 128)
    return lax.all_to_all(sent, ("az", "ax"), 0, 0, tiled=True).reshape(2 * devices, 128)


def per_device(layer_input, pre_act, out_grad, point_weight, spec_weight, saved_coeffs):
    axial_devices = lax.axis_size("ax")
    cycle_devices = lax.axis_size("az")
    devices = axial_devices * cycle_devices
    axial_total = layer_input.shape[1] * axial_devices
    cycle_total = layer_input.shape[2] * cycle_devices
    radial_length = layer_input.shape[3]
    cells_total = axial_total * cycle_total * radial_length
    gain = math.sqrt(cells_total / (2.0 * MX * MT * MR))
    norm = 1.0 / math.sqrt(cells_total)
    tables = make_tables(axial_total, cycle_total, radial_length, cycle_devices)

    grad_pre, sent = first(layer_input, pre_act, out_grad, tables)
    got = exchange(sent, devices)
    mode_grad, sent = middle(got, spec_weight, tables, gain, norm)
    got = exchange(sent.reshape(2 * devices, 128), devices)
    saved_modes = saved_coeffs.reshape(MX, CH).astype(F32)
    spec_grad = (
        (saved_modes[:, :, None] * mode_grad[:, :CH].astype(F32)[:, None, :]).astype(BF).reshape(1, MX, CH * CH)
    )
    inverse, _ = lax.optimization_barrier((tables["inverse"], mode_grad))
    inverse = lax.dynamic_index_in_dim(inverse, lax.axis_index("az"), 0, keepdims=False)
    point_part = jnp.einsum("io,oxtr->ixtr", point_weight, grad_pre, preferred_element_type=F32)
    input_grad, point_grad, bias_rows = last(got, inverse, point_part, tables)
    return (input_grad, point_grad, bias_rows[0, :CH], spec_grad)


def solution(mesh):
    return jax.shard_map(
        per_device,
        mesh=mesh,
        in_specs=(
            P(None, "ax", "az", None),
            P(None, "ax", "az", None),
            P(None, "ax", "az", None),
            P(),
            P(("az", "ax"), None, None),
            P(("az", "ax"), None),
        ),
        out_specs=(P(None, "ax", "az", None), P(), P(), P(("az", "ax"), None, None)),
        check_vma=False,
    )
```

```python
import functools
import math

import jax
import jax.numpy as jnp
import numpy as np
from jax import lax
from jax.experimental import pallas as pl
from jax.experimental.pallas import tpu as pltpu
from jax.sharding import PartitionSpec as P

CH = 64
MX = 32
MT = 16
MR = 16
BF = jnp.bfloat16
F32 = jnp.float32
VMEM_LIMIT = 48 * 1024 * 1024


def cosine_table(extent, wanted):
    places = np.arange(extent) + 0.5
    orders = np.arange(wanted)
    table = math.sqrt(2.0 / extent) * np.cos(math.pi * places[:, None] * orders[None, :] / extent)
    table[:, 0] *= 1.0 / math.sqrt(2.0)
    return table.astype(np.float32).astype(jnp.bfloat16).astype(np.float32)


def cycle_table(extent, half_modes):
    angles = 2.0 * math.pi * (np.arange(extent) + 0.5) / extent
    orders = np.arange(half_modes)
    cosines = math.sqrt(2.0 / extent) * np.cos(angles[:, None] * orders[None, :])
    cosines[:, 0] *= 1.0 / math.sqrt(2.0)
    sines = math.sqrt(2.0 / extent) * np.sin(angles[:, None] * (orders[None, :] + 1.0))
    table = np.concatenate([cosines, sines], axis=1)
    return table.astype(np.float32).astype(jnp.bfloat16).astype(np.float32)


def make_tables(axial, cycle, radial, cycle_devices):
    sector = cycle // cycle_devices
    pairs = 2 * MT * MR
    radial_table, axial_table = cosine_table(radial, MR), cosine_table(axial, MX)
    cycle_all = cycle_table(cycle, MT)
    tables = {}
    swap = np.zeros((16, 16, 16, 16), np.float32)
    for a in range(16):
        for b in range(16):
            swap[a, b, b, a] = 1.0
    tables["swap"] = swap.reshape(256, 256)
    ends = np.zeros((32, radial), np.float32)
    ends[:MR] = radial_table.T
    ends[MR:] = 1.0
    tables["ends"] = ends
    forward = np.zeros((cycle_devices, 2 * MT, MR, 2, sector, MR), np.float32)
    for k in range(MR):
        part = cycle_all.reshape(cycle_devices, sector, 2 * MT)
        forward[:, :, k, 0, :, k] = part.transpose(0, 2, 1)
    forward = forward.reshape(cycle_devices, 2 * pairs, sector * MR)
    tables["forward"] = forward
    tables["inverse"] = forward.transpose(0, 2, 1)
    rows = np.zeros((pairs, 2, 128), np.float32)
    for p in range(pairs):
        rows[p, 1, CH if p % 8 == 7 else p // 8] = 1.0
    tables["place"] = rows.reshape(2 * pairs, 128)
    pick = np.zeros((80, pairs, 2), np.float32)
    for i in range(CH):
        pick[i, 8 * i, 1] = 1.0
    pick[CH, 7, 1] = 1.0
    tables["pick"] = pick.reshape(80, 2 * pairs)
    gather = np.zeros((80, cycle_devices, pairs // cycle_devices, 2), np.float32)
    ax_devices = pairs // cycle_devices
    slab = axial // ax_devices
    by_slab = axial_table.reshape(ax_devices, slab, MX)
    gather[: slab * MX, :, :, 0] = by_slab.transpose(1, 2, 0).reshape(slab * MX, 1, ax_devices)
    gather[slab * MX :, :, :, 1] = 1.0
    tables["gather"] = gather.reshape(80, 2 * pairs)
    spread = np.zeros((ax_devices, 2, slab * MX), np.float32)
    spread[:, 0, :] = by_slab.reshape(ax_devices, slab * MX)
    tables["spread"] = spread.reshape(2 * ax_devices, slab * MX)
    halves = (np.arange(128)[:, None] // 64 == np.arange(128)[None, :] // 64).astype(np.float32)
    tables["halves"] = np.concatenate([halves, halves], axis=0)
    tables["radial"] = np.tile(radial_table.T, (sector, 1))
    tables["same"] = (np.arange(sector * MR)[None, :] // MR == np.arange(sector)[:, None]).astype(np.float32)
    return {name: value.astype(jnp.float32 if name == "same" else jnp.bfloat16) for name, value in tables.items()}


def gelu_slope(values):
    density = jnp.exp(-0.5 * values * values) * (1.0 / math.sqrt(2.0 * math.pi))
    return 0.5 * (1.0 + lax.erf(values * (1.0 / math.sqrt(2.0)))) + values * density


def dot_nn(a, b):
    return lax.dot_general(a, b, (((1,), (0,)), ((), ())), preferred_element_type=F32)


def dot_nt(a, b):
    return lax.dot_general(a, b, (((1,), (1,)), ((), ())), preferred_element_type=F32)


def split_halves(values):
    lane = lax.broadcasted_iota(jnp.int32, values.shape, 1)
    high = values.astype(BF).astype(F32)
    return jnp.where(lane < 64, high, pltpu.roll(values - high, 64, 1))


def first_kernel(where, swap_ref, ends_ref, layer_hbm, pre_hbm, grad_hbm, place_hbm, forward_hbm,
                 slope_hbm, sent_ref, layer, pre, grad, slope, layer_rows, grad_rows, coefs, place, forward,
                 in_sem, out_sem, table_sem):
    chunks = in_sem.shape[0]
    group = CH // chunks
    copies = []
    for c in range(chunks):
        part = pl.ds(c * group, group)
        pairs = ((pre_hbm, pre), (grad_hbm, grad), (layer_hbm, layer))
        copies.append([pltpu.make_async_copy(a.at[part], b.at[part], in_sem.at[c, n]) for n, (a, b) in enumerate(pairs)])
        for copy in copies[-1]:
            copy.start()
    tables = [
        pltpu.make_async_copy(forward_hbm.at[where[0]], forward, table_sem.at[0]),
        pltpu.make_async_copy(place_hbm, place, table_sem.at[1]),
    ]
    for copy in tables:
        copy.start()
    swap = swap_ref[...]
    leaving = []
    for c in range(chunks):
        part = pl.ds(c * group, group)
        for copy in copies[c]:
            copy.wait()
        slope[part] = (grad[part].astype(F32) * gelu_slope(pre[part].astype(F32))).astype(BF)
        leaving.append(pltpu.make_async_copy(slope.at[part], slope_hbm.at[part], out_sem.at[c]))
        leaving[-1].start()
        for at in range(c * group, (c + 1) * group, 16):
            for x in range(2):
                both = jnp.concatenate(
                    [layer[at : at + 16, x].reshape(256, 128), slope[at : at + 16, x].reshape(256, 128)], axis=1
                )
                moved = dot_nn(swap, both).astype(BF)
                rows = slice(x * CH + at, x * CH + at + 16)
                layer_rows[:, rows, :] = moved[:, :128].reshape(16, 16, 128)
                grad_rows[:, rows, :] = moved[:, 128:].reshape(16, 16, 128)
    point = jnp.zeros((128, 128), F32)
    bias = jnp.zeros((16, 128), F32)
    for t in range(16):
        left = jnp.concatenate([layer_rows[t], ends_ref[...]], axis=0)
        out = dot_nt(left, grad_rows[t])
        point += out[:128]
        coefs[t * MR : (t + 1) * MR, :] = out[128:144].astype(BF)
        bias += out[144:]
    point = point[:64] + pltpu.roll(point[64:], 64, 1)
    bias = bias + pltpu.roll(bias, 64, 1)
    sums = jnp.concatenate([split_halves(point), split_halves(bias), jnp.zeros((48, 128), F32)], axis=0)
    for copy in tables:
        copy.wait()
    sent = dot_nn(forward[...], coefs[...]) + dot_nn(place[...], sums.astype(BF))
    sent_ref[...] = sent.astype(BF)
    for copy in leaving:
        copy.wait()


def first(layer_input, pre_act, out_grad, tables):
    chunks = 2
    shape = (CH, 2, 16, 128)
    where = lax.axis_index("az").astype(jnp.int32).reshape(1)
    hbm, vmem = pl.BlockSpec(memory_space=pl.ANY), pl.BlockSpec(memory_space=pltpu.VMEM)
    return pl.pallas_call(
        first_kernel,
        in_specs=[pl.BlockSpec(memory_space=pltpu.SMEM), vmem, vmem, hbm, hbm, hbm, hbm, hbm],
        out_specs=[hbm, vmem],
        scratch_shapes=[
            pltpu.VMEM(shape, BF),
            pltpu.VMEM(shape, BF),
            pltpu.VMEM(shape, BF),
            pltpu.VMEM(shape, BF),
            pltpu.VMEM((16, 128, 128), BF),
            pltpu.VMEM((16, 128, 128), BF),
            pltpu.VMEM((256, 128), BF),
            pltpu.VMEM((1024, 128), BF),
            pltpu.VMEM((1024, 256), BF),
            pltpu.SemaphoreType.DMA((chunks, 3)),
            pltpu.SemaphoreType.DMA((chunks,)),
            pltpu.SemaphoreType.DMA((2,)),
        ],
        out_shape=[jax.ShapeDtypeStruct(shape, BF), jax.ShapeDtypeStruct((1024, 128), BF)],
        compiler_params=pltpu.CompilerParams(vmem_limit_bytes=60 * 1024 * 1024),
        name="slope_and_modes",
    )(where, tables["swap"], tables["ends"], layer_input, pre_act, out_grad, tables["place"], tables["forward"])


def middle_kernel(gain, norm, got_ref, gather_ref, weight_ref, halves_ref, spread_ref, mode_ref, sent_ref, stack):
    full = dot_nn(gather_ref[...], got_ref[...])
    lane = lax.broadcasted_iota(jnp.int32, (32, 128), 1)
    picked = jnp.where(lane < 64, full[:32], full[32:64])
    mode = (gain * (picked + pltpu.roll(picked, 64, 1))).astype(BF)
    mode_ref[...] = mode
    mode_wide = mode.astype(F32)
    for c in range(32):
        product = weight_ref[0, :, c * 128 : (c + 1) * 128].astype(F32) * mode_wide
        high = product.astype(BF)
        stack[c * 32 : (c + 1) * 32, :128] = high
        stack[c * 32 : (c + 1) * 32, 128:] = (product - high.astype(F32)).astype(BF)
    summed = dot_nn(stack[...], halves_ref[...])
    coef = jnp.zeros((32, 128), F32)
    for c in range(32):
        coef = jnp.where(lane % 64 == c, summed[c * 32 : (c + 1) * 32], coef)
    coef = jnp.concatenate([coef, pltpu.roll(coef, 32, 1)], axis=0).astype(BF)
    slabs = dot_nn(spread_ref[...], coef)
    sums = full[64:80]
    sums = split_halves((sums + pltpu.roll(sums, 64, 1)) * norm)
    row = lax.broadcasted_iota(jnp.int32, (128, 128), 0)
    slabs = jnp.where(row % 2 == 0, slabs, sums[:1]).astype(BF)
    for az in range(8):
        sent_ref[az] = slabs


def middle(got, spec_weight, tables, gain, norm):
    return pl.pallas_call(
        functools.partial(middle_kernel, gain, norm),
        out_shape=[jax.ShapeDtypeStruct((32, 128), BF), jax.ShapeDtypeStruct((8, 128, 128), BF)],
        scratch_shapes=[pltpu.VMEM((1024, 256), BF)],
        compiler_params=pltpu.CompilerParams(vmem_limit_bytes=VMEM_LIMIT),
        name="modes_and_mixing",
    )(got, tables["gather"], spec_weight, tables["halves"], tables["spread"])


def last_kernel(got_ref, pick_ref, radial_ref, same_ref, inverse_ref, point_ref,
                field_hbm, weight_ref, bias_ref, columns, wide, field, out_sem):
    got = got_ref[...]
    columns[...] = jnp.transpose(dot_nn(inverse_ref[...], got))
    same = same_ref[...]
    radial = radial_ref[...]
    chunks = out_sem.shape[0]
    group = CH // chunks
    leaving = []
    for c in range(chunks):
        for at in range(group):
            for x in range(2):
                i = c * group + at
                place = (i % 2) * 64 + x * 32 + i // 2
                value = jnp.broadcast_to(columns[place : place + 1, :], (16, 256)) * same
                wide[c, (at * 2 + x) * 16 : (at * 2 + x) * 16 + 16, :] = value.astype(BF)
        part = slice(c * group, (c + 1) * group)
        spectral = dot_nn(wide[c], radial)
        field[part] = (spectral.reshape(group, 2, 16, 128) + point_ref[part]).astype(BF)
        leaving.append(pltpu.make_async_copy(field.at[part], field_hbm.at[part], out_sem.at[c]))
        leaving[-1].start()
    sums = dot_nn(pick_ref[...], got)
    sums = sums + pltpu.roll(sums, 64, 1)
    weight_ref[...] = sums[:64, :64]
    bias_ref[...] = sums[64, :64]
    for copy in leaving:
        copy.wait()


def last(got, inverse, point_part, tables):
    chunks = 4
    shape = (CH, 2, 16, 128)
    hbm, vmem = pl.BlockSpec(memory_space=pl.ANY), pl.BlockSpec(memory_space=pltpu.VMEM)
    return pl.pallas_call(
        last_kernel,
        in_specs=[vmem] * 6,
        out_specs=[hbm, vmem, vmem],
        scratch_shapes=[
            pltpu.VMEM((128, 256), F32),
            pltpu.VMEM((chunks, CH // chunks * 32, 256), BF),
            pltpu.VMEM(shape, BF),
            pltpu.SemaphoreType.DMA((chunks,)),
        ],
        out_shape=[
            jax.ShapeDtypeStruct(shape, BF),
            jax.ShapeDtypeStruct((CH, CH), F32),
            jax.ShapeDtypeStruct((CH,), F32),
        ],
        compiler_params=pltpu.CompilerParams(vmem_limit_bytes=32 * 1024 * 1024),
        name="modes_to_field",
    )(got, tables["pick"], tables["radial"], tables["same"], inverse, point_part)


def exchange(rows, devices):
    sent = rows.reshape(devices, 2, 128)
    return lax.all_to_all(sent, ("az", "ax"), 0, 0, tiled=True).reshape(2 * devices, 128)


def per_device(layer_input, pre_act, out_grad, point_weight, spec_weight, saved_coeffs):
    axial_devices = lax.axis_size("ax")
    cycle_devices = lax.axis_size("az")
    devices = axial_devices * cycle_devices
    axial_total = layer_input.shape[1] * axial_devices
    cycle_total = layer_input.shape[2] * cycle_devices
    radial_length = layer_input.shape[3]
    cells_total = axial_total * cycle_total * radial_length
    gain = math.sqrt(cells_total / (2.0 * MX * MT * MR))
    norm = 1.0 / math.sqrt(cells_total)
    tables = make_tables(axial_total, cycle_total, radial_length, cycle_devices)

    grad_pre, sent = first(layer_input, pre_act, out_grad, tables)
    got = exchange(sent, devices)
    mode_grad, sent = middle(got, spec_weight, tables, gain, norm)
    got = exchange(sent.reshape(2 * devices, 128), devices)
    saved_modes = saved_coeffs.reshape(MX, CH).astype(F32)
    spec_grad = (
        (saved_modes[:, :, None] * mode_grad[:, :CH].astype(F32)[:, None, :]).astype(BF).reshape(1, MX, CH * CH)
    )
    inverse, _ = lax.optimization_barrier((tables["inverse"], mode_grad))
    inverse = lax.dynamic_index_in_dim(inverse, lax.axis_index("az"), 0, keepdims=False)
    point_part = jnp.einsum("io,oxtr->ixtr", point_weight, grad_pre, preferred_element_type=F32)
    input_grad, point_grad, bias_grad = last(got, inverse, point_part, tables)
    return (input_grad, point_grad, bias_grad, spec_grad)


def solution(mesh):
    return jax.shard_map(
        per_device,
        mesh=mesh,
        in_specs=(
            P(None, "ax", "az", None),
            P(None, "ax", "az", None),
            P(None, "ax", "az", None),
            P(),
            P(("az", "ax"), None, None),
            P(("az", "ax"), None),
        ),
        out_specs=(P(None, "ax", "az", None), P(), P(), P(("az", "ax"), None, None)),
        check_vma=False,
    )
```

```python
import functools
import math

import jax
import jax.numpy as jnp
import numpy as np
from jax import lax
from jax.experimental import pallas as pl
from jax.experimental.pallas import tpu as pltpu
from jax.sharding import PartitionSpec as P

CH = 64
MX = 32
MT = 16
MR = 16
BF = jnp.bfloat16
F32 = jnp.float32
VMEM_LIMIT = 48 * 1024 * 1024


def cosine_table(extent, wanted):
    places = np.arange(extent) + 0.5
    orders = np.arange(wanted)
    table = math.sqrt(2.0 / extent) * np.cos(math.pi * places[:, None] * orders[None, :] / extent)
    table[:, 0] *= 1.0 / math.sqrt(2.0)
    return table.astype(np.float32).astype(jnp.bfloat16).astype(np.float32)


def cycle_table(extent, half_modes):
    angles = 2.0 * math.pi * (np.arange(extent) + 0.5) / extent
    orders = np.arange(half_modes)
    cosines = math.sqrt(2.0 / extent) * np.cos(angles[:, None] * orders[None, :])
    cosines[:, 0] *= 1.0 / math.sqrt(2.0)
    sines = math.sqrt(2.0 / extent) * np.sin(angles[:, None] * (orders[None, :] + 1.0))
    table = np.concatenate([cosines, sines], axis=1)
    return table.astype(np.float32).astype(jnp.bfloat16).astype(np.float32)


def make_tables(axial, cycle, radial, cycle_devices):
    sector = cycle // cycle_devices
    pairs = 2 * MT * MR
    radial_table, axial_table = cosine_table(radial, MR), cosine_table(axial, MX)
    cycle_all = cycle_table(cycle, MT)
    tables = {}
    swap = np.zeros((16, 16, 16, 16), np.float32)
    for a in range(16):
        for b in range(16):
            swap[a, b, b, a] = 1.0
    tables["swap"] = swap.reshape(256, 256)
    ends = np.zeros((32, radial), np.float32)
    ends[:MR] = radial_table.T
    ends[MR:] = 1.0
    tables["ends"] = ends
    forward = np.zeros((cycle_devices, 2 * MT, MR, 2, sector, MR), np.float32)
    for k in range(MR):
        part = cycle_all.reshape(cycle_devices, sector, 2 * MT)
        forward[:, :, k, 0, :, k] = part.transpose(0, 2, 1)
    forward = forward.reshape(cycle_devices, 2 * pairs, sector * MR)
    tables["forward"] = forward
    tables["inverse"] = forward.transpose(0, 2, 1)
    rows = np.zeros((pairs, 2, 128), np.float32)
    for p in range(pairs):
        rows[p, 1, CH if p % 8 == 7 else p // 8] = 1.0
    tables["place"] = rows.reshape(2 * pairs, 128)
    pick = np.zeros((80, pairs, 2), np.float32)
    for i in range(CH):
        pick[i, 8 * i, 1] = 1.0
    pick[CH, 7, 1] = 1.0
    tables["pick"] = pick.reshape(80, 2 * pairs)
    gather = np.zeros((80, cycle_devices, pairs // cycle_devices, 2), np.float32)
    ax_devices = pairs // cycle_devices
    slab = axial // ax_devices
    by_slab = axial_table.reshape(ax_devices, slab, MX)
    gather[: slab * MX, :, :, 0] = by_slab.transpose(1, 2, 0).reshape(slab * MX, 1, ax_devices)
    gather[slab * MX :, :, :, 1] = 1.0
    tables["gather"] = gather.reshape(80, 2 * pairs)
    spread = np.zeros((ax_devices, 2, slab * MX), np.float32)
    spread[:, 0, :] = by_slab.reshape(ax_devices, slab * MX)
    tables["spread"] = spread.reshape(2 * ax_devices, slab * MX)
    halves = (np.arange(128)[:, None] // 64 == np.arange(128)[None, :] // 64).astype(np.float32)
    tables["halves"] = np.concatenate([halves, halves], axis=0)
    tables["radial"] = np.tile(radial_table.T, (sector, 1))
    tables["same"] = (np.arange(sector * MR)[None, :] // MR == np.arange(sector)[:, None]).astype(np.float32)
    return {name: value.astype(jnp.float32 if name == "same" else jnp.bfloat16) for name, value in tables.items()}


def gelu_slope(values):
    density = jnp.exp(-0.5 * values * values) * (1.0 / math.sqrt(2.0 * math.pi))
    return 0.5 * (1.0 + lax.erf(values * (1.0 / math.sqrt(2.0)))) + values * density


def dot_nn(a, b):
    return lax.dot_general(a, b, (((1,), (0,)), ((), ())), preferred_element_type=F32)


def dot_nt(a, b):
    return lax.dot_general(a, b, (((1,), (1,)), ((), ())), preferred_element_type=F32)


def split_halves(values):
    lane = lax.broadcasted_iota(jnp.int32, values.shape, 1)
    high = values.astype(BF).astype(F32)
    return jnp.where(lane < 64, high, pltpu.roll(values - high, 64, 1))


def first_kernel(layer_hbm, pre_hbm, grad_hbm, swap_hbm, ends_hbm, place_hbm, forward_hbm,
                 slope_hbm, sent_hbm, layer, pre, grad, slope, layer_rows, grad_rows, coefs,
                 swap, ends, place, forward, sent, in_sem, out_sem, table_sem, sent_sem):
    chunks, blocks = in_sem.shape[0], sent_sem.shape[0]
    group, size = CH // chunks, sent.shape[0] // blocks
    copies = []
    for c in range(chunks):
        part = pl.ds(c * group, group)
        pairs = ((pre_hbm, pre), (grad_hbm, grad), (layer_hbm, layer))
        copies.append([pltpu.make_async_copy(a.at[part], b.at[part], in_sem.at[c, n]) for n, (a, b) in enumerate(pairs)])
    pairs = ((swap_hbm, swap), (ends_hbm, ends), (place_hbm, place), (forward_hbm.at[lax.axis_index("az")], forward))
    tables = [pltpu.make_async_copy(a, b, table_sem.at[n]) for n, (a, b) in enumerate(pairs)]
    for copy in copies[0] + tables[:1] + sum(copies[1:], []) + tables[1:]:
        copy.start()
    leaving = []
    for c in range(chunks):
        part = pl.ds(c * group, group)
        copies[c][0].wait()
        copies[c][1].wait()
        slope[part] = (grad[part].astype(F32) * gelu_slope(pre[part].astype(F32))).astype(BF)
        leaving.append(pltpu.make_async_copy(slope.at[part], slope_hbm.at[part], out_sem.at[c]))
        leaving[-1].start()
        copies[c][2].wait()
        if c == 0:
            tables[0].wait()
        for at in range(c * group, (c + 1) * group, 16):
            for x in range(2):
                both = jnp.concatenate(
                    [layer[at : at + 16, x].reshape(256, 128), slope[at : at + 16, x].reshape(256, 128)], axis=1
                )
                moved = dot_nn(swap[...], both).astype(BF)
                rows = slice(x * CH + at, x * CH + at + 16)
                layer_rows[:, rows, :] = moved[:, :128].reshape(16, 16, 128)
                grad_rows[:, rows, :] = moved[:, 128:].reshape(16, 16, 128)
    for copy in tables[1:]:
        copy.wait()
    point = jnp.zeros((128, 128), F32)
    bias = jnp.zeros((16, 128), F32)
    for t in range(16):
        left = jnp.concatenate([layer_rows[t], ends[...]], axis=0)
        out = dot_nt(left, grad_rows[t])
        point += out[:128]
        coefs[t * MR : (t + 1) * MR, :] = out[128:144].astype(BF)
        bias += out[144:]
    point = point[:64] + pltpu.roll(point[64:], 64, 1)
    bias = bias + pltpu.roll(bias, 64, 1)
    sums = jnp.concatenate([split_halves(point), split_halves(bias), jnp.zeros((48, 128), F32)], axis=0).astype(BF)
    coef = coefs[...]
    for b in range(blocks):
        rows = slice(b * size, (b + 1) * size)
        sent[rows] = (dot_nn(forward[rows], coef) + dot_nn(place[rows], sums)).astype(BF)
        leaving.append(pltpu.make_async_copy(sent.at[rows], sent_hbm.at[rows], sent_sem.at[b]))
        leaving[-1].start()
    for copy in leaving:
        copy.wait()


def first(layer_input, pre_act, out_grad, tables):
    chunks, blocks = 2, 2
    shape = (CH, 2, 16, 128)
    hbm = pl.BlockSpec(memory_space=pl.ANY)
    return pl.pallas_call(
        first_kernel,
        in_specs=[hbm] * 7,
        out_specs=[hbm] * 2,
        scratch_shapes=[pltpu.VMEM(shape, BF)] * 4
        + [
            pltpu.VMEM((16, 128, 128), BF),
            pltpu.VMEM((16, 128, 128), BF),
            pltpu.VMEM((256, 128), BF),
            pltpu.VMEM((256, 256), BF),
            pltpu.VMEM((32, 128), BF),
            pltpu.VMEM((1024, 128), BF),
            pltpu.VMEM((1024, 256), BF),
            pltpu.VMEM((1024, 128), BF),
            pltpu.SemaphoreType.DMA((chunks, 3)),
            pltpu.SemaphoreType.DMA((chunks,)),
            pltpu.SemaphoreType.DMA((4,)),
            pltpu.SemaphoreType.DMA((blocks,)),
        ],
        out_shape=[jax.ShapeDtypeStruct(shape, BF), jax.ShapeDtypeStruct((1024, 128), BF)],
        compiler_params=pltpu.CompilerParams(vmem_limit_bytes=60 * 1024 * 1024),
        name="slope_and_modes",
    )(layer_input, pre_act, out_grad, tables["swap"], tables["ends"], tables["place"], tables["forward"])


def middle_kernel(gain, norm, got_ref, gather_ref, weight_ref, halves_ref, spread_ref, mode_ref, sent_ref, stack):
    full = dot_nn(gather_ref[...], got_ref[...])
    lane = lax.broadcasted_iota(jnp.int32, (32, 128), 1)
    picked = jnp.where(lane < 64, full[:32], full[32:64])
    mode = (gain * (picked + pltpu.roll(picked, 64, 1))).astype(BF)
    mode_ref[...] = mode
    mode_wide = mode.astype(F32)
    for c in range(32):
        product = weight_ref[0, :, c * 128 : (c + 1) * 128].astype(F32) * mode_wide
        high = product.astype(BF)
        stack[c * 32 : (c + 1) * 32, :128] = high
        stack[c * 32 : (c + 1) * 32, 128:] = (product - high.astype(F32)).astype(BF)
    summed = dot_nn(stack[...], halves_ref[...])
    coef = jnp.zeros((32, 128), F32)
    for c in range(32):
        coef = jnp.where(lane % 64 == c, summed[c * 32 : (c + 1) * 32], coef)
    coef = jnp.concatenate([coef, pltpu.roll(coef, 32, 1)], axis=0).astype(BF)
    slabs = dot_nn(spread_ref[...], coef)
    sums = full[64:80]
    sums = split_halves((sums + pltpu.roll(sums, 64, 1)) * norm)
    row = lax.broadcasted_iota(jnp.int32, (128, 128), 0)
    slabs = jnp.where(row % 2 == 0, slabs, sums[:1]).astype(BF)
    for az in range(8):
        sent_ref[az] = slabs


def middle(got, spec_weight, tables, gain, norm):
    return pl.pallas_call(
        functools.partial(middle_kernel, gain, norm),
        out_shape=[jax.ShapeDtypeStruct((32, 128), BF), jax.ShapeDtypeStruct((8, 128, 128), BF)],
        scratch_shapes=[pltpu.VMEM((1024, 256), BF)],
        compiler_params=pltpu.CompilerParams(vmem_limit_bytes=VMEM_LIMIT),
        name="modes_and_mixing",
    )(got, tables["gather"], spec_weight, tables["halves"], tables["spread"])


def last_kernel(got_ref, pick_ref, radial_ref, same_ref, inverse_ref, point_ref,
                field_hbm, weight_hbm, bias_hbm, columns, wide, field, weight, bias, out_sem, sums_sem):
    got = got_ref[...]
    sums = dot_nn(pick_ref[...], got)
    sums = sums + pltpu.roll(sums, 64, 1)
    weight[...] = sums[:64, :64]
    bias[...] = sums[64, :64]
    leaving = [
        pltpu.make_async_copy(weight, weight_hbm, sums_sem.at[0]),
        pltpu.make_async_copy(bias, bias_hbm, sums_sem.at[1]),
    ]
    for copy in leaving:
        copy.start()
    columns[...] = jnp.transpose(dot_nn(inverse_ref[...], got))
    same = same_ref[...]
    radial = radial_ref[...]
    chunks = out_sem.shape[0]
    group = CH // chunks
    for c in range(chunks):
        for at in range(group):
            for x in range(2):
                i = c * group + at
                place = (i % 2) * 64 + x * 32 + i // 2
                value = jnp.broadcast_to(columns[place : place + 1, :], (16, 256)) * same
                wide[c, (at * 2 + x) * 16 : (at * 2 + x) * 16 + 16, :] = value.astype(BF)
        part = slice(c * group, (c + 1) * group)
        spectral = dot_nn(wide[c], radial)
        field[part] = (spectral.reshape(group, 2, 16, 128) + point_ref[part]).astype(BF)
        leaving.append(pltpu.make_async_copy(field.at[part], field_hbm.at[part], out_sem.at[c]))
        leaving[-1].start()
    for copy in leaving:
        copy.wait()


def last(got, inverse, point_part, tables):
    chunks = 4
    shape = (CH, 2, 16, 128)
    hbm, vmem = pl.BlockSpec(memory_space=pl.ANY), pl.BlockSpec(memory_space=pltpu.VMEM)
    return pl.pallas_call(
        last_kernel,
        in_specs=[vmem] * 6,
        out_specs=[hbm] * 3,
        scratch_shapes=[
            pltpu.VMEM((128, 256), F32),
            pltpu.VMEM((chunks, CH // chunks * 32, 256), BF),
            pltpu.VMEM(shape, BF),
            pltpu.VMEM((CH, CH), F32),
            pltpu.VMEM((CH,), F32),
            pltpu.SemaphoreType.DMA((chunks,)),
            pltpu.SemaphoreType.DMA((2,)),
        ],
        out_shape=[
            jax.ShapeDtypeStruct(shape, BF),
            jax.ShapeDtypeStruct((CH, CH), F32),
            jax.ShapeDtypeStruct((CH,), F32),
        ],
        compiler_params=pltpu.CompilerParams(vmem_limit_bytes=32 * 1024 * 1024),
        name="modes_to_field",
    )(got, tables["pick"], tables["radial"], tables["same"], inverse, point_part)


def exchange(rows, devices):
    sent = rows.reshape(devices, 2, 128)
    return lax.all_to_all(sent, ("az", "ax"), 0, 0, tiled=True).reshape(2 * devices, 128)


def per_device(layer_input, pre_act, out_grad, point_weight, spec_weight, saved_coeffs):
    axial_devices = lax.axis_size("ax")
    cycle_devices = lax.axis_size("az")
    devices = axial_devices * cycle_devices
    axial_total = layer_input.shape[1] * axial_devices
    cycle_total = layer_input.shape[2] * cycle_devices
    radial_length = layer_input.shape[3]
    cells_total = axial_total * cycle_total * radial_length
    gain = math.sqrt(cells_total / (2.0 * MX * MT * MR))
    norm = 1.0 / math.sqrt(cells_total)
    tables = make_tables(axial_total, cycle_total, radial_length, cycle_devices)

    grad_pre, sent = first(layer_input, pre_act, out_grad, tables)
    got = exchange(sent, devices)
    mode_grad, sent = middle(got, spec_weight, tables, gain, norm)
    got = exchange(sent.reshape(2 * devices, 128), devices)
    saved_modes = saved_coeffs.reshape(MX, CH).astype(F32)
    spec_grad = (
        (saved_modes[:, :, None] * mode_grad[:, :CH].astype(F32)[:, None, :]).astype(BF).reshape(1, MX, CH * CH)
    )
    inverse, _ = lax.optimization_barrier((tables["inverse"], mode_grad))
    inverse = lax.dynamic_index_in_dim(inverse, lax.axis_index("az"), 0, keepdims=False)
    point_part = jnp.einsum("io,oxtr->ixtr", point_weight, grad_pre, preferred_element_type=F32)
    input_grad, point_grad, bias_grad = last(got, inverse, point_part, tables)
    return (input_grad, point_grad, bias_grad, spec_grad)


def solution(mesh):
    return jax.shard_map(
        per_device,
        mesh=mesh,
        in_specs=(
            P(None, "ax", "az", None),
            P(None, "ax", "az", None),
            P(None, "ax", "az", None),
            P(),
            P(("az", "ax"), None, None),
            P(("az", "ax"), None),
        ),
        out_specs=(P(None, "ax", "az", None), P(), P(), P(("az", "ax"), None, None)),
        check_vma=False,
    )
```

```python
import functools
import math

import jax
import jax.numpy as jnp
import numpy as np
from jax import lax
from jax.experimental import pallas as pl
from jax.experimental.pallas import tpu as pltpu
from jax.sharding import Mesh
from jax.sharding import PartitionSpec as P

CH = 64
MX = 32
MT = 16
MR = 16
BF = jnp.bfloat16
F32 = jnp.float32
VMEM_LIMIT = 48 * 1024 * 1024


def cosine_table(extent, wanted):
    places = np.arange(extent) + 0.5
    orders = np.arange(wanted)
    table = math.sqrt(2.0 / extent) * np.cos(math.pi * places[:, None] * orders[None, :] / extent)
    table[:, 0] *= 1.0 / math.sqrt(2.0)
    return table.astype(np.float32).astype(jnp.bfloat16).astype(np.float32)


def cycle_table(extent, half_modes):
    angles = 2.0 * math.pi * (np.arange(extent) + 0.5) / extent
    orders = np.arange(half_modes)
    cosines = math.sqrt(2.0 / extent) * np.cos(angles[:, None] * orders[None, :])
    cosines[:, 0] *= 1.0 / math.sqrt(2.0)
    sines = math.sqrt(2.0 / extent) * np.sin(angles[:, None] * (orders[None, :] + 1.0))
    table = np.concatenate([cosines, sines], axis=1)
    return table.astype(np.float32).astype(jnp.bfloat16).astype(np.float32)


def make_tables(axial, cycle, radial, cycle_devices):
    sector = cycle // cycle_devices
    pairs = 2 * MT * MR
    radial_table, axial_table = cosine_table(radial, MR), cosine_table(axial, MX)
    cycle_all = cycle_table(cycle, MT)
    tables = {}
    swap = np.zeros((16, 16, 16, 16), np.float32)
    for a in range(16):
        for b in range(16):
            swap[a, b, b, a] = 1.0
    tables["swap"] = swap.reshape(256, 256)
    ends = np.zeros((32, radial), np.float32)
    ends[:MR] = radial_table.T
    ends[MR:] = 1.0
    tables["ends"] = ends
    forward = np.zeros((cycle_devices, 2 * MT, MR, 2, sector, MR), np.float32)
    for k in range(MR):
        part = cycle_all.reshape(cycle_devices, sector, 2 * MT)
        forward[:, :, k, 0, :, k] = part.transpose(0, 2, 1)
    forward = forward.reshape(cycle_devices, 2 * pairs, sector * MR)
    tables["forward"] = forward
    rows = np.zeros((pairs, 2, 128), np.float32)
    for p in range(pairs):
        rows[p, 1, CH if p % 8 == 7 else p // 8] = 1.0
    tables["place"] = rows.reshape(2 * pairs, 128)
    pick = np.zeros((80, pairs, 2), np.float32)
    for i in range(CH):
        pick[i, 8 * i, 1] = 1.0
    pick[CH, 7, 1] = 1.0
    inverse = np.concatenate(
        [forward.transpose(0, 2, 1), np.broadcast_to(pick.reshape(1, 80, 2 * pairs), (cycle_devices, 80, 2 * pairs))], axis=1
    )
    inverse = inverse.reshape(cycle_devices, 336, cycle_devices // 2, 2, 2 * pairs // cycle_devices)
    inverse = np.stack([inverse[az][:, :, [az % 2, 1 - az % 2]] for az in range(cycle_devices)])
    tables["inverse"] = inverse.transpose(0, 1, 3, 2, 4).reshape(cycle_devices, 336, 2 * pairs)
    gather = np.zeros((80, cycle_devices, pairs // cycle_devices, 2), np.float32)
    ax_devices = pairs // cycle_devices
    slab = axial // ax_devices
    by_slab = axial_table.reshape(ax_devices, slab, MX)
    gather[: slab * MX, :, :, 0] = by_slab.transpose(1, 2, 0).reshape(slab * MX, 1, ax_devices)
    gather[slab * MX :, :, :, 1] = 1.0
    tables["gather"] = gather.reshape(80, 2 * pairs)
    spread = np.zeros((ax_devices, 2, slab * MX), np.float32)
    spread[:, 0, :] = by_slab.reshape(ax_devices, slab * MX)
    tables["spread"] = spread.reshape(2 * ax_devices, slab * MX)
    halves = (np.arange(128)[:, None] // 64 == np.arange(128)[None, :] // 64).astype(np.float32)
    tables["halves"] = np.concatenate([halves, halves], axis=0)
    tables["radial"] = np.tile(radial_table.T, (sector, 1))
    tables["same"] = (np.arange(sector * MR)[None, :] // MR == np.arange(sector)[:, None]).astype(np.float32)
    return {name: value.astype(jnp.float32 if name == "same" else jnp.bfloat16) for name, value in tables.items()}


def cycle_index():
    return lax.axis_index("y_hi") * 2 + lax.axis_index("core")


def gelu_slope(values):
    density = jnp.exp(-0.5 * values * values) * (1.0 / math.sqrt(2.0 * math.pi))
    return 0.5 * (1.0 + lax.erf(values * (1.0 / math.sqrt(2.0)))) + values * density


def dot_nn(a, b):
    return lax.dot_general(a, b, (((1,), (0,)), ((), ())), preferred_element_type=F32)


def dot_nt(a, b):
    return lax.dot_general(a, b, (((1,), (1,)), ((), ())), preferred_element_type=F32)


def split_halves(values):
    lane = lax.broadcasted_iota(jnp.int32, values.shape, 1)
    high = values.astype(BF).astype(F32)
    return jnp.where(lane < 64, high, pltpu.roll(values - high, 64, 1))


def first_kernel(layer_hbm, pre_hbm, grad_hbm, swap_hbm, ends_hbm, place_hbm, forward_hbm,
                 slope_hbm, sent_hbm, layer, pre, grad, slope, layer_rows, grad_rows, coefs,
                 swap, ends, place, forward, sent, in_sem, out_sem, table_sem, sent_sem):
    chunks, blocks = in_sem.shape[0], sent_sem.shape[0]
    group, size = CH // chunks, sent.shape[0] // blocks
    copies = []
    for c in range(chunks):
        part = pl.ds(c * group, group)
        pairs = ((pre_hbm, pre), (grad_hbm, grad), (layer_hbm, layer))
        copies.append([pltpu.make_async_copy(a.at[part], b.at[part], in_sem.at[c, n]) for n, (a, b) in enumerate(pairs)])
    pairs = ((swap_hbm, swap), (ends_hbm, ends), (place_hbm, place), (forward_hbm.at[cycle_index()], forward))
    tables = [pltpu.make_async_copy(a, b, table_sem.at[n]) for n, (a, b) in enumerate(pairs)]
    for copy in copies[0] + tables[:1] + sum(copies[1:], []) + tables[1:]:
        copy.start()
    leaving = []
    for c in range(chunks):
        part = pl.ds(c * group, group)
        copies[c][0].wait()
        copies[c][1].wait()
        slope[part] = (grad[part].astype(F32) * gelu_slope(pre[part].astype(F32))).astype(BF)
        leaving.append(pltpu.make_async_copy(slope.at[part], slope_hbm.at[part], out_sem.at[c]))
        leaving[-1].start()
        copies[c][2].wait()
        if c == 0:
            tables[0].wait()
        for at in range(c * group, (c + 1) * group, 16):
            for x in range(2):
                both = jnp.concatenate(
                    [layer[at : at + 16, x].reshape(256, 128), slope[at : at + 16, x].reshape(256, 128)], axis=1
                )
                moved = dot_nn(swap[...], both).astype(BF)
                rows = slice(x * CH + at, x * CH + at + 16)
                layer_rows[:, rows, :] = moved[:, :128].reshape(16, 16, 128)
                grad_rows[:, rows, :] = moved[:, 128:].reshape(16, 16, 128)
    for copy in tables[1:]:
        copy.wait()
    point = jnp.zeros((128, 128), F32)
    bias = jnp.zeros((16, 128), F32)
    for t in range(16):
        left = jnp.concatenate([layer_rows[t], ends[...]], axis=0)
        out = dot_nt(left, grad_rows[t])
        point += out[:128]
        coefs[t * MR : (t + 1) * MR, :] = out[128:144].astype(BF)
        bias += out[144:]
    point = point[:64] + pltpu.roll(point[64:], 64, 1)
    bias = bias + pltpu.roll(bias, 64, 1)
    sums = jnp.concatenate([split_halves(point), split_halves(bias), jnp.zeros((48, 128), F32)], axis=0).astype(BF)
    coef = coefs[...]
    for b in range(blocks):
        rows = slice(b * size, (b + 1) * size)
        sent[rows] = (dot_nn(forward[rows], coef) + dot_nn(place[rows], sums)).astype(BF)
        leaving.append(pltpu.make_async_copy(sent.at[rows], sent_hbm.at[rows], sent_sem.at[b]))
        leaving[-1].start()
    for copy in leaving:
        copy.wait()


def first(layer_input, pre_act, out_grad, tables):
    chunks, blocks = 2, 2
    shape = (CH, 2, 16, 128)
    hbm = pl.BlockSpec(memory_space=pl.ANY)
    return pl.pallas_call(
        first_kernel,
        in_specs=[hbm] * 7,
        out_specs=[hbm] * 2,
        scratch_shapes=[pltpu.VMEM(shape, BF)] * 4
        + [
            pltpu.VMEM((16, 128, 128), BF),
            pltpu.VMEM((16, 128, 128), BF),
            pltpu.VMEM((256, 128), BF),
            pltpu.VMEM((256, 256), BF),
            pltpu.VMEM((32, 128), BF),
            pltpu.VMEM((1024, 128), BF),
            pltpu.VMEM((1024, 256), BF),
            pltpu.VMEM((1024, 128), BF),
            pltpu.SemaphoreType.DMA((chunks, 3)),
            pltpu.SemaphoreType.DMA((chunks,)),
            pltpu.SemaphoreType.DMA((4,)),
            pltpu.SemaphoreType.DMA((blocks,)),
        ],
        out_shape=[jax.ShapeDtypeStruct(shape, BF), jax.ShapeDtypeStruct((1024, 128), BF)],
        compiler_params=pltpu.CompilerParams(vmem_limit_bytes=60 * 1024 * 1024),
        name="slope_and_modes",
    )(layer_input, pre_act, out_grad, tables["swap"], tables["ends"], tables["place"], tables["forward"])


def middle_kernel(gain, norm, got_ref, gather_ref, weight_ref, halves_ref, spread_ref, mode_ref, sent_ref, stack):
    full = dot_nn(gather_ref[...], got_ref[...])
    lane = lax.broadcasted_iota(jnp.int32, (32, 128), 1)
    picked = jnp.where(lane < 64, full[:32], full[32:64])
    mode = (gain * (picked + pltpu.roll(picked, 64, 1))).astype(BF)
    mode_ref[...] = mode
    mode_wide = mode.astype(F32)
    for c in range(32):
        product = weight_ref[0, :, c * 128 : (c + 1) * 128].astype(F32) * mode_wide
        high = product.astype(BF)
        stack[c * 32 : (c + 1) * 32, :128] = high
        stack[c * 32 : (c + 1) * 32, 128:] = (product - high.astype(F32)).astype(BF)
    summed = dot_nn(stack[...], halves_ref[...])
    coef = jnp.zeros((32, 128), F32)
    for c in range(32):
        coef = jnp.where(lane % 64 == c, summed[c * 32 : (c + 1) * 32], coef)
    coef = jnp.concatenate([coef, pltpu.roll(coef, 32, 1)], axis=0).astype(BF)
    slabs = dot_nn(spread_ref[...], coef)
    sums = full[64:80]
    sums = split_halves((sums + pltpu.roll(sums, 64, 1)) * norm)
    row = lax.broadcasted_iota(jnp.int32, (128, 128), 0)
    slabs = jnp.where(row % 2 == 0, slabs, sums[:1]).astype(BF)
    for y_hi in range(4):
        sent_ref[y_hi] = slabs


def middle(got, spec_weight, tables, gain, norm):
    return pl.pallas_call(
        functools.partial(middle_kernel, gain, norm),
        out_shape=[jax.ShapeDtypeStruct((32, 128), BF), jax.ShapeDtypeStruct((4, 128, 128), BF)],
        scratch_shapes=[pltpu.VMEM((1024, 256), BF)],
        compiler_params=pltpu.CompilerParams(vmem_limit_bytes=VMEM_LIMIT),
        name="modes_and_mixing",
    )(got, tables["gather"], spec_weight, tables["halves"], tables["spread"])


def last_kernel(own_ref, other_ref, radial_ref, same_ref, inverse_ref, point_ref,
                field_hbm, weight_hbm, bias_hbm, columns, wide, field, weight, bias, out_sem, sums_sem):
    half = own_ref.shape[0]
    out = dot_nn(inverse_ref[:, :half], own_ref[...]) + dot_nn(inverse_ref[:, half:], other_ref[...])
    sums = out[256:] + pltpu.roll(out[256:], 64, 1)
    weight[...] = sums[:64, :64]
    bias[...] = sums[64, :64]
    leaving = [
        pltpu.make_async_copy(weight, weight_hbm, sums_sem.at[0]),
        pltpu.make_async_copy(bias, bias_hbm, sums_sem.at[1]),
    ]
    for copy in leaving:
        copy.start()
    columns[...] = jnp.transpose(out[:256])
    same = same_ref[...]
    radial = radial_ref[...]
    chunks = out_sem.shape[0]
    group = CH // chunks
    for c in range(chunks):
        for at in range(group):
            for x in range(2):
                i = c * group + at
                place = (i % 2) * 64 + x * 32 + i // 2
                value = jnp.broadcast_to(columns[place : place + 1, :], (16, 256)) * same
                wide[c, (at * 2 + x) * 16 : (at * 2 + x) * 16 + 16, :] = value.astype(BF)
        part = slice(c * group, (c + 1) * group)
        spectral = dot_nn(wide[c], radial)
        field[part] = (spectral.reshape(group, 2, 16, 128) + point_ref[part]).astype(BF)
        leaving.append(pltpu.make_async_copy(field.at[part], field_hbm.at[part], out_sem.at[c]))
        leaving[-1].start()
    for copy in leaving:
        copy.wait()


def last(own, other, inverse, point_part, tables):
    chunks = 4
    shape = (CH, 2, 16, 128)
    hbm, vmem = pl.BlockSpec(memory_space=pl.ANY), pl.BlockSpec(memory_space=pltpu.VMEM)
    return pl.pallas_call(
        last_kernel,
        in_specs=[vmem] * 6,
        out_specs=[hbm] * 3,
        scratch_shapes=[
            pltpu.VMEM((128, 256), F32),
            pltpu.VMEM((chunks, CH // chunks * 32, 256), BF),
            pltpu.VMEM(shape, BF),
            pltpu.VMEM((CH, CH), F32),
            pltpu.VMEM((CH,), F32),
            pltpu.SemaphoreType.DMA((chunks,)),
            pltpu.SemaphoreType.DMA((2,)),
        ],
        out_shape=[
            jax.ShapeDtypeStruct(shape, BF),
            jax.ShapeDtypeStruct((CH, CH), F32),
            jax.ShapeDtypeStruct((CH,), F32),
        ],
        compiler_params=pltpu.CompilerParams(vmem_limit_bytes=32 * 1024 * 1024),
        name="modes_to_field",
    )(own, other, tables["radial"], tables["same"], inverse, point_part)


def exchange(rows, axes):
    sent = rows.reshape(-1, 2, 128)
    return lax.all_to_all(sent, axes, 0, 0, tiled=True).reshape(-1, 128)


def per_device(layer_input, pre_act, out_grad, point_weight, spec_weight, saved_coeffs):
    axial_devices = lax.axis_size("ax")
    cycle_devices = lax.axis_size(("y_hi", "core"))
    axial_total = layer_input.shape[1] * axial_devices
    cycle_total = layer_input.shape[2] * cycle_devices
    radial_length = layer_input.shape[3]
    cells_total = axial_total * cycle_total * radial_length
    gain = math.sqrt(cells_total / (2.0 * MX * MT * MR))
    norm = 1.0 / math.sqrt(cells_total)
    tables = make_tables(axial_total, cycle_total, radial_length, cycle_devices)

    grad_pre, sent = first(layer_input, pre_act, out_grad, tables)
    got = exchange(sent, ("y_hi", "core", "ax"))
    mode_grad, sent = middle(got, spec_weight, tables, gain, norm)
    own = exchange(sent, ("y_hi", "ax"))
    saved_modes = saved_coeffs.reshape(MX, CH).astype(F32)
    spec_grad = (
        (saved_modes[:, :, None] * mode_grad[:, :CH].astype(F32)[:, None, :]).astype(BF).reshape(1, MX, CH * CH)
    )
    inverse, _ = lax.optimization_barrier((tables["inverse"], mode_grad))
    inverse = lax.dynamic_index_in_dim(inverse, cycle_index(), 0, keepdims=False)
    point_part = jnp.einsum("io,oxtr->ixtr", point_weight, grad_pre, preferred_element_type=F32)
    own, inverse, point_part, spec_grad = lax.optimization_barrier((own, inverse, point_part, spec_grad))
    other = lax.ppermute(own, "core", [(0, 1), (1, 0)])
    input_grad, point_grad, bias_grad = last(own, other, inverse, point_part, tables)
    return (input_grad, point_grad, bias_grad, spec_grad)


def solution(mesh):
    by_core = Mesh(mesh.devices.reshape(mesh.devices.shape[0], -1, 2), ("ax", "y_hi", "core"))
    field = P(None, "ax", ("y_hi", "core"), None)
    return jax.shard_map(
        per_device,
        mesh=by_core,
        in_specs=(field, field, field, P(), P(("y_hi", "core", "ax"), None, None), P(("y_hi", "core", "ax"), None)),
        out_specs=(field, P(), P(), P(("y_hi", "core", "ax"), None, None)),
        check_vma=False,
    )
```

```python
import functools
import math

import jax
import jax.numpy as jnp
import numpy as np
from jax import lax
from jax.experimental import pallas as pl
from jax.experimental.pallas import tpu as pltpu
from jax.sharding import PartitionSpec as P

CH = 64
MX = 32
MT = 16
MR = 16
BF = jnp.bfloat16
F32 = jnp.float32
VMEM_LIMIT = 48 * 1024 * 1024


def cosine_table(extent, wanted):
    places = np.arange(extent) + 0.5
    orders = np.arange(wanted)
    table = math.sqrt(2.0 / extent) * np.cos(math.pi * places[:, None] * orders[None, :] / extent)
    table[:, 0] *= 1.0 / math.sqrt(2.0)
    return table.astype(np.float32).astype(jnp.bfloat16).astype(np.float32)


def cycle_table(extent, half_modes):
    angles = 2.0 * math.pi * (np.arange(extent) + 0.5) / extent
    orders = np.arange(half_modes)
    cosines = math.sqrt(2.0 / extent) * np.cos(angles[:, None] * orders[None, :])
    cosines[:, 0] *= 1.0 / math.sqrt(2.0)
    sines = math.sqrt(2.0 / extent) * np.sin(angles[:, None] * (orders[None, :] + 1.0))
    table = np.concatenate([cosines, sines], axis=1)
    return table.astype(np.float32).astype(jnp.bfloat16).astype(np.float32)


def make_tables(axial, cycle, radial, cycle_devices):
    sector = cycle // cycle_devices
    pairs = 2 * MT * MR
    radial_table, axial_table = cosine_table(radial, MR), cosine_table(axial, MX)
    cycle_all = cycle_table(cycle, MT)
    tables = {}
    swap = np.zeros((16, 16, 16, 16), np.float32)
    for a in range(16):
        for b in range(16):
            swap[a, b, b, a] = 1.0
    tables["swap"] = swap.reshape(256, 256)
    ends = np.zeros((32, radial), np.float32)
    ends[:MR] = radial_table.T
    ends[MR:] = 1.0
    tables["ends"] = ends
    forward = np.zeros((cycle_devices, 2 * MT, MR, 2, sector, MR), np.float32)
    for k in range(MR):
        part = cycle_all.reshape(cycle_devices, sector, 2 * MT)
        forward[:, :, k, 0, :, k] = part.transpose(0, 2, 1)
    forward = forward.reshape(cycle_devices, 2 * pairs, sector * MR)
    tables["inverse"] = forward.transpose(0, 2, 1)
    rows = np.zeros((pairs, 2, 128), np.float32)
    for p in range(pairs):
        rows[p, 1, CH if p % 8 == 7 else p // 8] = 1.0
    place = np.broadcast_to(rows.reshape(1, 2 * pairs, 128), (cycle_devices, 2 * pairs, 128))
    tables["forward"] = np.concatenate([forward, place], axis=2)
    pick = np.zeros((80, pairs, 2), np.float32)
    for i in range(CH):
        pick[i, 8 * i, 1] = 1.0
    pick[CH, 7, 1] = 1.0
    tables["pick"] = pick.reshape(80, 2 * pairs)
    gather = np.zeros((80, cycle_devices, pairs // cycle_devices, 2), np.float32)
    ax_devices = pairs // cycle_devices
    slab = axial // ax_devices
    by_slab = axial_table.reshape(ax_devices, slab, MX)
    gather[: slab * MX, :, :, 0] = by_slab.transpose(1, 2, 0).reshape(slab * MX, 1, ax_devices)
    gather[slab * MX :, :, :, 1] = 1.0
    tables["gather"] = gather.reshape(80, 2 * pairs)
    spread = np.zeros((ax_devices, 2, slab * MX), np.float32)
    spread[:, 0, :] = by_slab.reshape(ax_devices, slab * MX)
    tables["spread"] = spread.reshape(2 * ax_devices, slab * MX)
    halves = (np.arange(128)[:, None] // 64 == np.arange(128)[None, :] // 64).astype(np.float32)
    tables["halves"] = np.concatenate([halves, halves], axis=0)
    tables["radial"] = np.tile(radial_table.T, (sector, 1))
    tables["same"] = (np.arange(sector * MR)[None, :] // MR == np.arange(sector)[:, None]).astype(np.float32)
    return {name: value.astype(jnp.float32 if name == "same" else jnp.bfloat16) for name, value in tables.items()}


def gelu_slope(values):
    density = jnp.exp(-0.5 * values * values) * (1.0 / math.sqrt(2.0 * math.pi))
    return 0.5 * (1.0 + lax.erf(values * (1.0 / math.sqrt(2.0)))) + values * density


def dot_nn(a, b):
    return lax.dot_general(a, b, (((1,), (0,)), ((), ())), preferred_element_type=F32)


def dot_nt(a, b):
    return lax.dot_general(a, b, (((1,), (1,)), ((), ())), preferred_element_type=F32)


def split_halves(values):
    lane = lax.broadcasted_iota(jnp.int32, values.shape, 1)
    high = values.astype(BF).astype(F32)
    return jnp.where(lane < 64, high, pltpu.roll(values - high, 64, 1))


def first_kernel(layer_hbm, pre_hbm, grad_hbm, swap_hbm, ends_hbm, forward_hbm,
                 slope_hbm, sent_hbm, layer, pre, grad, slope, layer_rows, grad_rows, coefs,
                 swap, ends, forward, sent, in_sem, out_sem, table_sem, sent_sem):
    chunks, blocks = in_sem.shape[0], sent_sem.shape[0]
    group, size = CH // chunks, sent.shape[0] // blocks
    copies = []
    for c in range(chunks):
        part = pl.ds(c * group, group)
        pairs = ((pre_hbm, pre), (grad_hbm, grad), (layer_hbm, layer))
        copies.append([pltpu.make_async_copy(a.at[part], b.at[part], in_sem.at[c, n]) for n, (a, b) in enumerate(pairs)])
    pairs = ((swap_hbm, swap), (ends_hbm, ends), (forward_hbm.at[lax.axis_index("az")], forward))
    tables = [pltpu.make_async_copy(a, b, table_sem.at[n]) for n, (a, b) in enumerate(pairs)]
    for copy in copies[0] + tables[:1] + sum(copies[1:], []) + tables[1:]:
        copy.start()
    leaving = []
    for c in range(chunks):
        part = pl.ds(c * group, group)
        copies[c][0].wait()
        copies[c][1].wait()
        slope[part] = (grad[part].astype(F32) * gelu_slope(pre[part].astype(F32))).astype(BF)
        leaving.append(pltpu.make_async_copy(slope.at[part], slope_hbm.at[part], out_sem.at[c]))
        leaving[-1].start()
        copies[c][2].wait()
        if c == 0:
            tables[0].wait()
        for at in range(c * group, (c + 1) * group, 16):
            for x in range(2):
                both = jnp.concatenate(
                    [layer[at : at + 16, x].reshape(256, 128), slope[at : at + 16, x].reshape(256, 128)], axis=1
                )
                moved = dot_nn(swap[...], both).astype(BF)
                rows = slice(x * CH + at, x * CH + at + 16)
                layer_rows[:, rows, :] = moved[:, :128].reshape(16, 16, 128)
                grad_rows[:, rows, :] = moved[:, 128:].reshape(16, 16, 128)
    for copy in tables[1:]:
        copy.wait()
    point = dot_nt(
        jnp.concatenate([layer_rows[t] for t in range(16)], axis=1), jnp.concatenate([grad_rows[t] for t in range(16)], axis=1)
    )
    out = dot_nt(ends[...], grad_rows[...].reshape(2048, 128))
    bias = jnp.zeros((16, 128), F32)
    for t in range(16):
        coefs[t * MR : (t + 1) * MR, :] = out[:16, t * 128 : (t + 1) * 128].astype(BF)
        bias += out[16:, t * 128 : (t + 1) * 128]
    point = point[:64] + pltpu.roll(point[64:], 64, 1)
    bias = bias + pltpu.roll(bias, 64, 1)
    sums = jnp.concatenate([split_halves(point), split_halves(bias), jnp.zeros((48, 128), F32)], axis=0).astype(BF)
    coef = jnp.concatenate([coefs[...], sums], axis=0)
    for b in range(blocks):
        rows = slice(b * size, (b + 1) * size)
        sent[rows] = dot_nn(forward[rows], coef).astype(BF)
        leaving.append(pltpu.make_async_copy(sent.at[rows], sent_hbm.at[rows], sent_sem.at[b]))
        leaving[-1].start()
    for copy in leaving:
        copy.wait()


def first(layer_input, pre_act, out_grad, tables):
    chunks, blocks = 2, 2
    shape = (CH, 2, 16, 128)
    hbm = pl.BlockSpec(memory_space=pl.ANY)
    return pl.pallas_call(
        first_kernel,
        in_specs=[hbm] * 6,
        out_specs=[hbm] * 2,
        scratch_shapes=[pltpu.VMEM(shape, BF)] * 4
        + [
            pltpu.VMEM((16, 128, 128), BF),
            pltpu.VMEM((16, 128, 128), BF),
            pltpu.VMEM((256, 128), BF),
            pltpu.VMEM((256, 256), BF),
            pltpu.VMEM((32, 128), BF),
            pltpu.VMEM((1024, 384), BF),
            pltpu.VMEM((1024, 128), BF),
            pltpu.SemaphoreType.DMA((chunks, 3)),
            pltpu.SemaphoreType.DMA((chunks,)),
            pltpu.SemaphoreType.DMA((3,)),
            pltpu.SemaphoreType.DMA((blocks,)),
        ],
        out_shape=[jax.ShapeDtypeStruct(shape, BF), jax.ShapeDtypeStruct((1024, 128), BF)],
        compiler_params=pltpu.CompilerParams(vmem_limit_bytes=60 * 1024 * 1024),
        name="slope_and_modes",
    )(layer_input, pre_act, out_grad, tables["swap"], tables["ends"], tables["forward"])


def middle_kernel(gain, norm, got_ref, gather_ref, weight_ref, halves_ref, spread_ref, mode_ref, sent_ref, stack):
    full = dot_nn(gather_ref[...], got_ref[...])
    lane = lax.broadcasted_iota(jnp.int32, (32, 128), 1)
    picked = jnp.where(lane < 64, full[:32], full[32:64])
    mode = (gain * (picked + pltpu.roll(picked, 64, 1))).astype(BF)
    mode_ref[...] = mode
    mode_wide = mode.astype(F32)
    for c in range(32):
        product = weight_ref[0, :, c * 128 : (c + 1) * 128].astype(F32) * mode_wide
        high = product.astype(BF)
        stack[c * 32 : (c + 1) * 32, :128] = high
        stack[c * 32 : (c + 1) * 32, 128:] = (product - high.astype(F32)).astype(BF)
    summed = dot_nn(stack[...], halves_ref[...])
    coef = jnp.zeros((32, 128), F32)
    for c in range(32):
        coef = jnp.where(lane % 64 == c, summed[c * 32 : (c + 1) * 32], coef)
    coef = jnp.concatenate([coef, pltpu.roll(coef, 32, 1)], axis=0).astype(BF)
    slabs = dot_nn(spread_ref[...], coef)
    sums = full[64:80]
    sums = split_halves((sums + pltpu.roll(sums, 64, 1)) * norm)
    row = lax.broadcasted_iota(jnp.int32, (128, 128), 0)
    slabs = jnp.where(row % 2 == 0, slabs, sums[:1]).astype(BF)
    for az in range(8):
        sent_ref[az] = slabs


def middle(got, spec_weight, tables, gain, norm):
    return pl.pallas_call(
        functools.partial(middle_kernel, gain, norm),
        out_shape=[jax.ShapeDtypeStruct((32, 128), BF), jax.ShapeDtypeStruct((8, 128, 128), BF)],
        scratch_shapes=[pltpu.VMEM((1024, 256), BF)],
        compiler_params=pltpu.CompilerParams(vmem_limit_bytes=VMEM_LIMIT),
        name="modes_and_mixing",
    )(got, tables["gather"], spec_weight, tables["halves"], tables["spread"])


def last_kernel(got_ref, pick_ref, radial_ref, same_ref, inverse_ref, point_ref,
                field_hbm, weight_hbm, bias_hbm, columns, wide, field, weight, bias, out_sem, sums_sem):
    got = got_ref[...]
    sums = dot_nn(pick_ref[...], got)
    sums = sums + pltpu.roll(sums, 64, 1)
    weight[...] = sums[:64, :64]
    bias[...] = sums[64, :64]
    leaving = [
        pltpu.make_async_copy(weight, weight_hbm, sums_sem.at[0]),
        pltpu.make_async_copy(bias, bias_hbm, sums_sem.at[1]),
    ]
    for copy in leaving:
        copy.start()
    columns[...] = jnp.transpose(dot_nn(inverse_ref[...], got))
    same = same_ref[...]
    radial = radial_ref[...]
    chunks = out_sem.shape[0]
    group = CH // chunks
    for c in range(chunks):
        for at in range(group):
            for x in range(2):
                i = c * group + at
                place = (i % 2) * 64 + x * 32 + i // 2
                value = jnp.broadcast_to(columns[place : place + 1, :], (16, 256)) * same
                wide[c, (at * 2 + x) * 16 : (at * 2 + x) * 16 + 16, :] = value.astype(BF)
        part = slice(c * group, (c + 1) * group)
        spectral = dot_nn(wide[c], radial)
        field[part] = (spectral.reshape(group, 2, 16, 128) + point_ref[part]).astype(BF)
        leaving.append(pltpu.make_async_copy(field.at[part], field_hbm.at[part], out_sem.at[c]))
        leaving[-1].start()
    for copy in leaving:
        copy.wait()


def last(got, inverse, point_part, tables):
    chunks = 4
    shape = (CH, 2, 16, 128)
    hbm, vmem = pl.BlockSpec(memory_space=pl.ANY), pl.BlockSpec(memory_space=pltpu.VMEM)
    return pl.pallas_call(
        last_kernel,
        in_specs=[vmem] * 6,
        out_specs=[hbm] * 3,
        scratch_shapes=[
            pltpu.VMEM((128, 256), F32),
            pltpu.VMEM((chunks, CH // chunks * 32, 256), BF),
            pltpu.VMEM(shape, BF),
            pltpu.VMEM((CH, CH), F32),
            pltpu.VMEM((CH,), F32),
            pltpu.SemaphoreType.DMA((chunks,)),
            pltpu.SemaphoreType.DMA((2,)),
        ],
        out_shape=[
            jax.ShapeDtypeStruct(shape, BF),
            jax.ShapeDtypeStruct((CH, CH), F32),
            jax.ShapeDtypeStruct((CH,), F32),
        ],
        compiler_params=pltpu.CompilerParams(vmem_limit_bytes=32 * 1024 * 1024),
        name="modes_to_field",
    )(got, tables["pick"], tables["radial"], tables["same"], inverse, point_part)


def exchange(rows, devices):
    sent = rows.reshape(devices, 2, 128)
    return lax.all_to_all(sent, ("az", "ax"), 0, 0, tiled=True).reshape(2 * devices, 128)


def per_device(layer_input, pre_act, out_grad, point_weight, spec_weight, saved_coeffs):
    axial_devices = lax.axis_size("ax")
    cycle_devices = lax.axis_size("az")
    devices = axial_devices * cycle_devices
    axial_total = layer_input.shape[1] * axial_devices
    cycle_total = layer_input.shape[2] * cycle_devices
    radial_length = layer_input.shape[3]
    cells_total = axial_total * cycle_total * radial_length
    gain = math.sqrt(cells_total / (2.0 * MX * MT * MR))
    norm = 1.0 / math.sqrt(cells_total)
    tables = make_tables(axial_total, cycle_total, radial_length, cycle_devices)

    grad_pre, sent = first(layer_input, pre_act, out_grad, tables)
    got = exchange(sent, devices)
    mode_grad, sent = middle(got, spec_weight, tables, gain, norm)
    got = exchange(sent.reshape(2 * devices, 128), devices)
    saved_modes = saved_coeffs.reshape(MX, CH).astype(F32)
    spec_grad = (
        (saved_modes[:, :, None] * mode_grad[:, :CH].astype(F32)[:, None, :]).astype(BF).reshape(1, MX, CH * CH)
    )
    inverse, _ = lax.optimization_barrier((tables["inverse"], mode_grad))
    inverse = lax.dynamic_index_in_dim(inverse, lax.axis_index("az"), 0, keepdims=False)
    point_part = jnp.einsum("io,oxtr->ixtr", point_weight, grad_pre, preferred_element_type=F32)
    input_grad, point_grad, bias_grad = last(got, inverse, point_part, tables)
    return (input_grad, point_grad, bias_grad, spec_grad)


def solution(mesh):
    return jax.shard_map(
        per_device,
        mesh=mesh,
        in_specs=(
            P(None, "ax", "az", None),
            P(None, "ax", "az", None),
            P(None, "ax", "az", None),
            P(),
            P(("az", "ax"), None, None),
            P(("az", "ax"), None),
        ),
        out_specs=(P(None, "ax", "az", None), P(), P(), P(("az", "ax"), None, None)),
        check_vma=False,
    )
```

```python
import functools
import math

import jax
import jax.numpy as jnp
import numpy as np
from jax import lax
from jax.experimental import pallas as pl
from jax.experimental.pallas import tpu as pltpu
from jax.sharding import PartitionSpec as P

CH = 64
MX = 32
MT = 16
MR = 16
BF = jnp.bfloat16
F32 = jnp.float32
VMEM_LIMIT = 48 * 1024 * 1024


def cosine_table(extent, wanted):
    places = np.arange(extent) + 0.5
    orders = np.arange(wanted)
    table = math.sqrt(2.0 / extent) * np.cos(math.pi * places[:, None] * orders[None, :] / extent)
    table[:, 0] *= 1.0 / math.sqrt(2.0)
    return table.astype(np.float32).astype(jnp.bfloat16).astype(np.float32)


def cycle_table(extent, half_modes):
    angles = 2.0 * math.pi * (np.arange(extent) + 0.5) / extent
    orders = np.arange(half_modes)
    cosines = math.sqrt(2.0 / extent) * np.cos(angles[:, None] * orders[None, :])
    cosines[:, 0] *= 1.0 / math.sqrt(2.0)
    sines = math.sqrt(2.0 / extent) * np.sin(angles[:, None] * (orders[None, :] + 1.0))
    table = np.concatenate([cosines, sines], axis=1)
    return table.astype(np.float32).astype(jnp.bfloat16).astype(np.float32)


def make_tables(axial, cycle, radial, cycle_devices):
    sector = cycle // cycle_devices
    pairs = 2 * MT * MR
    radial_table, axial_table = cosine_table(radial, MR), cosine_table(axial, MX)
    cycle_all = cycle_table(cycle, MT)
    tables = {}
    ends = np.zeros((32, radial), np.float32)
    ends[:MR] = radial_table.T
    ends[MR:] = 1.0
    tables["ends"] = ends
    forward = np.zeros((cycle_devices, 2 * MT, MR, 2, sector, MR), np.float32)
    for k in range(MR):
        part = cycle_all.reshape(cycle_devices, sector, 2 * MT)
        forward[:, :, k, 0, :, k] = part.transpose(0, 2, 1)
    forward = forward.reshape(cycle_devices, 2 * pairs, sector * MR)
    tables["inverse"] = forward.transpose(0, 2, 1)
    rows = np.zeros((pairs, 2, 128), np.float32)
    for p in range(pairs):
        rows[p, 1, CH if p % 8 == 7 else p // 8] = 1.0
    place = np.broadcast_to(rows.reshape(1, 2 * pairs, 128), (cycle_devices, 2 * pairs, 128))
    tables["forward"] = np.concatenate([forward, place], axis=2)
    pick = np.zeros((80, pairs, 2), np.float32)
    for i in range(CH):
        pick[i, 8 * i, 1] = 1.0
    pick[CH, 7, 1] = 1.0
    tables["pick"] = pick.reshape(80, 2 * pairs)
    gather = np.zeros((80, cycle_devices, pairs // cycle_devices, 2), np.float32)
    ax_devices = pairs // cycle_devices
    slab = axial // ax_devices
    by_slab = axial_table.reshape(ax_devices, slab, MX)
    gather[: slab * MX, :, :, 0] = by_slab.transpose(1, 2, 0).reshape(slab * MX, 1, ax_devices)
    gather[slab * MX :, :, :, 1] = 1.0
    tables["gather"] = gather.reshape(80, 2 * pairs)
    spread = np.zeros((ax_devices, 2, slab * MX), np.float32)
    spread[:, 0, :] = by_slab.reshape(ax_devices, slab * MX)
    tables["spread"] = spread.reshape(2 * ax_devices, slab * MX)
    halves = (np.arange(128)[:, None] // 64 == np.arange(128)[None, :] // 64).astype(np.float32)
    tables["halves"] = np.concatenate([halves, halves], axis=0)
    tables["radial"] = np.tile(radial_table.T, (sector, 1))
    tables["same"] = (np.arange(sector * MR)[None, :] // MR == np.arange(sector)[:, None]).astype(np.float32)
    return {name: value.astype(jnp.float32 if name == "same" else jnp.bfloat16) for name, value in tables.items()}


def gelu_slope(values):
    density = jnp.exp(-0.5 * values * values) * (1.0 / math.sqrt(2.0 * math.pi))
    return 0.5 * (1.0 + lax.erf(values * (1.0 / math.sqrt(2.0)))) + values * density


def dot_nn(a, b):
    return lax.dot_general(a, b, (((1,), (0,)), ((), ())), preferred_element_type=F32)


def dot_nt(a, b):
    return lax.dot_general(a, b, (((1,), (1,)), ((), ())), preferred_element_type=F32)


def split_halves(values):
    lane = lax.broadcasted_iota(jnp.int32, values.shape, 1)
    high = values.astype(BF).astype(F32)
    return jnp.where(lane < 64, high, pltpu.roll(values - high, 64, 1))


def first_kernel(layer_hbm, pre_hbm, grad_hbm, ends_hbm, forward_hbm,
                 slope_hbm, sent_hbm, layer, pre, grad, slope, layer_rows, grad_rows, coefs,
                 ends, forward, sent, in_sem, out_sem, table_sem, sent_sem):
    chunks, blocks = in_sem.shape[0], sent_sem.shape[0]
    group, size = CH // chunks, sent.shape[0] // blocks
    copies = []
    for c in range(chunks):
        part = pl.ds(c * group, group)
        pairs = ((pre_hbm, pre), (grad_hbm, grad), (layer_hbm, layer))
        copies.append([pltpu.make_async_copy(a.at[part], b.at[part], in_sem.at[c, n]) for n, (a, b) in enumerate(pairs)])
    pairs = ((ends_hbm, ends), (forward_hbm.at[lax.axis_index("az")], forward))
    tables = [pltpu.make_async_copy(a, b, table_sem.at[n]) for n, (a, b) in enumerate(pairs)]
    for copy in sum(copies, []) + tables:
        copy.start()
    leaving = []
    for c in range(chunks):
        part = pl.ds(c * group, group)
        copies[c][0].wait()
        copies[c][1].wait()
        slope[part] = (grad[part].astype(F32) * gelu_slope(pre[part].astype(F32))).astype(BF)
        leaving.append(pltpu.make_async_copy(slope.at[part], slope_hbm.at[part], out_sem.at[c]))
        leaving[-1].start()
        copies[c][2].wait()
        for at in range(c * group, (c + 1) * group, 16):
            for x in range(2):
                rows = slice(x * CH + at, x * CH + at + 16)
                layer_rows[:, rows, :] = jnp.swapaxes(layer[at : at + 16, x], 0, 1)
                grad_rows[:, rows, :] = jnp.swapaxes(slope[at : at + 16, x], 0, 1)
    for copy in tables:
        copy.wait()
    point = dot_nt(
        jnp.concatenate([layer_rows[t] for t in range(16)], axis=1), jnp.concatenate([grad_rows[t] for t in range(16)], axis=1)
    )
    out = dot_nt(ends[...], grad_rows[...].reshape(2048, 128))
    bias = jnp.zeros((16, 128), F32)
    for t in range(16):
        coefs[t * MR : (t + 1) * MR, :] = out[:16, t * 128 : (t + 1) * 128].astype(BF)
        bias += out[16:, t * 128 : (t + 1) * 128]
    point = point[:64] + pltpu.roll(point[64:], 64, 1)
    bias = bias + pltpu.roll(bias, 64, 1)
    sums = jnp.concatenate([split_halves(point), split_halves(bias), jnp.zeros((48, 128), F32)], axis=0).astype(BF)
    coef = jnp.concatenate([coefs[...], sums], axis=0)
    for b in range(blocks):
        rows = slice(b * size, (b + 1) * size)
        sent[rows] = dot_nn(forward[rows], coef).astype(BF)
        leaving.append(pltpu.make_async_copy(sent.at[rows], sent_hbm.at[rows], sent_sem.at[b]))
        leaving[-1].start()
    for copy in leaving:
        copy.wait()


def first(layer_input, pre_act, out_grad, tables):
    chunks, blocks = 2, 2
    shape = (CH, 2, 16, 128)
    hbm = pl.BlockSpec(memory_space=pl.ANY)
    return pl.pallas_call(
        first_kernel,
        in_specs=[hbm] * 5,
        out_specs=[hbm] * 2,
        scratch_shapes=[pltpu.VMEM(shape, BF)] * 4
        + [
            pltpu.VMEM((16, 128, 128), BF),
            pltpu.VMEM((16, 128, 128), BF),
            pltpu.VMEM((256, 128), BF),
            pltpu.VMEM((32, 128), BF),
            pltpu.VMEM((1024, 384), BF),
            pltpu.VMEM((1024, 128), BF),
            pltpu.SemaphoreType.DMA((chunks, 3)),
            pltpu.SemaphoreType.DMA((chunks,)),
            pltpu.SemaphoreType.DMA((2,)),
            pltpu.SemaphoreType.DMA((blocks,)),
        ],
        out_shape=[jax.ShapeDtypeStruct(shape, BF), jax.ShapeDtypeStruct((1024, 128), BF)],
        compiler_params=pltpu.CompilerParams(vmem_limit_bytes=60 * 1024 * 1024),
        name="slope_and_modes",
    )(layer_input, pre_act, out_grad, tables["ends"], tables["forward"])


def middle_kernel(gain, norm, got_ref, gather_ref, weight_ref, halves_ref, spread_ref, mode_ref, sent_ref, stack):
    full = dot_nn(gather_ref[...], got_ref[...])
    lane = lax.broadcasted_iota(jnp.int32, (32, 128), 1)
    picked = jnp.where(lane < 64, full[:32], full[32:64])
    mode = (gain * (picked + pltpu.roll(picked, 64, 1))).astype(BF)
    mode_ref[...] = mode
    mode_wide = mode.astype(F32)
    for c in range(32):
        product = weight_ref[0, :, c * 128 : (c + 1) * 128].astype(F32) * mode_wide
        high = product.astype(BF)
        stack[c * 32 : (c + 1) * 32, :128] = high
        stack[c * 32 : (c + 1) * 32, 128:] = (product - high.astype(F32)).astype(BF)
    summed = dot_nn(stack[...], halves_ref[...])
    coef = jnp.zeros((32, 128), F32)
    for c in range(32):
        coef = jnp.where(lane % 64 == c, summed[c * 32 : (c + 1) * 32], coef)
    coef = jnp.concatenate([coef, pltpu.roll(coef, 32, 1)], axis=0).astype(BF)
    slabs = dot_nn(spread_ref[...], coef)
    sums = full[64:80]
    sums = split_halves((sums + pltpu.roll(sums, 64, 1)) * norm)
    row = lax.broadcasted_iota(jnp.int32, (128, 128), 0)
    slabs = jnp.where(row % 2 == 0, slabs, sums[:1]).astype(BF)
    for az in range(8):
        sent_ref[az] = slabs


def middle(got, spec_weight, tables, gain, norm):
    return pl.pallas_call(
        functools.partial(middle_kernel, gain, norm),
        out_shape=[jax.ShapeDtypeStruct((32, 128), BF), jax.ShapeDtypeStruct((8, 128, 128), BF)],
        scratch_shapes=[pltpu.VMEM((1024, 256), BF)],
        compiler_params=pltpu.CompilerParams(vmem_limit_bytes=VMEM_LIMIT),
        name="modes_and_mixing",
    )(got, tables["gather"], spec_weight, tables["halves"], tables["spread"])


def last_kernel(got_ref, pick_ref, radial_ref, same_ref, inverse_ref, point_ref,
                field_hbm, weight_hbm, bias_hbm, columns, wide, field, weight, bias, out_sem, sums_sem):
    got = got_ref[...]
    sums = dot_nn(pick_ref[...], got)
    sums = sums + pltpu.roll(sums, 64, 1)
    weight[...] = sums[:64, :64]
    bias[...] = sums[64, :64]
    leaving = [
        pltpu.make_async_copy(weight, weight_hbm, sums_sem.at[0]),
        pltpu.make_async_copy(bias, bias_hbm, sums_sem.at[1]),
    ]
    for copy in leaving:
        copy.start()
    columns[...] = jnp.transpose(dot_nn(inverse_ref[...], got))
    same = same_ref[...]
    radial = radial_ref[...]
    chunks = out_sem.shape[0]
    group = CH // chunks
    for c in range(chunks):
        for at in range(group):
            for x in range(2):
                i = c * group + at
                place = (i % 2) * 64 + x * 32 + i // 2
                value = jnp.broadcast_to(columns[place : place + 1, :], (16, 256)) * same
                wide[c, (at * 2 + x) * 16 : (at * 2 + x) * 16 + 16, :] = value.astype(BF)
        part = slice(c * group, (c + 1) * group)
        spectral = dot_nn(wide[c], radial)
        field[part] = (spectral.reshape(group, 2, 16, 128) + point_ref[part]).astype(BF)
        leaving.append(pltpu.make_async_copy(field.at[part], field_hbm.at[part], out_sem.at[c]))
        leaving[-1].start()
    for copy in leaving:
        copy.wait()


def last(got, inverse, point_part, tables):
    chunks = 4
    shape = (CH, 2, 16, 128)
    hbm, vmem = pl.BlockSpec(memory_space=pl.ANY), pl.BlockSpec(memory_space=pltpu.VMEM)
    return pl.pallas_call(
        last_kernel,
        in_specs=[vmem] * 6,
        out_specs=[hbm] * 3,
        scratch_shapes=[
            pltpu.VMEM((128, 256), F32),
            pltpu.VMEM((chunks, CH // chunks * 32, 256), BF),
            pltpu.VMEM(shape, BF),
            pltpu.VMEM((CH, CH), F32),
            pltpu.VMEM((CH,), F32),
            pltpu.SemaphoreType.DMA((chunks,)),
            pltpu.SemaphoreType.DMA((2,)),
        ],
        out_shape=[
            jax.ShapeDtypeStruct(shape, BF),
            jax.ShapeDtypeStruct((CH, CH), F32),
            jax.ShapeDtypeStruct((CH,), F32),
        ],
        compiler_params=pltpu.CompilerParams(vmem_limit_bytes=32 * 1024 * 1024),
        name="modes_to_field",
    )(got, tables["pick"], tables["radial"], tables["same"], inverse, point_part)


def exchange(rows, devices):
    sent = rows.reshape(devices, 2, 128)
    return lax.all_to_all(sent, ("az", "ax"), 0, 0, tiled=True).reshape(2 * devices, 128)


def per_device(layer_input, pre_act, out_grad, point_weight, spec_weight, saved_coeffs):
    axial_devices = lax.axis_size("ax")
    cycle_devices = lax.axis_size("az")
    devices = axial_devices * cycle_devices
    axial_total = layer_input.shape[1] * axial_devices
    cycle_total = layer_input.shape[2] * cycle_devices
    radial_length = layer_input.shape[3]
    cells_total = axial_total * cycle_total * radial_length
    gain = math.sqrt(cells_total / (2.0 * MX * MT * MR))
    norm = 1.0 / math.sqrt(cells_total)
    tables = make_tables(axial_total, cycle_total, radial_length, cycle_devices)

    grad_pre, sent = first(layer_input, pre_act, out_grad, tables)
    got = exchange(sent, devices)
    mode_grad, sent = middle(got, spec_weight, tables, gain, norm)
    got = exchange(sent.reshape(2 * devices, 128), devices)
    saved_modes = saved_coeffs.reshape(MX, CH).astype(F32)
    spec_grad = (
        (saved_modes[:, :, None] * mode_grad[:, :CH].astype(F32)[:, None, :]).astype(BF).reshape(1, MX, CH * CH)
    )
    inverse, _ = lax.optimization_barrier((tables["inverse"], mode_grad))
    inverse = lax.dynamic_index_in_dim(inverse, lax.axis_index("az"), 0, keepdims=False)
    point_part = jnp.einsum("io,oxtr->ixtr", point_weight, grad_pre, preferred_element_type=F32)
    input_grad, point_grad, bias_grad = last(got, inverse, point_part, tables)
    return (input_grad, point_grad, bias_grad, spec_grad)


def solution(mesh):
    return jax.shard_map(
        per_device,
        mesh=mesh,
        in_specs=(
            P(None, "ax", "az", None),
            P(None, "ax", "az", None),
            P(None, "ax", "az", None),
            P(),
            P(("az", "ax"), None, None),
            P(("az", "ax"), None),
        ),
        out_specs=(P(None, "ax", "az", None), P(), P(), P(("az", "ax"), None, None)),
        check_vma=False,
    )
```

```python
import functools
import math

import jax
import jax.numpy as jnp
import numpy as np
from jax import lax
from jax.experimental import pallas as pl
from jax.experimental.pallas import tpu as pltpu
from jax.sharding import PartitionSpec as P

CH = 64
MX = 32
MT = 16
MR = 16
BF = jnp.bfloat16
F32 = jnp.float32
VMEM_LIMIT = 48 * 1024 * 1024


def cosine_table(extent, wanted):
    places = np.arange(extent) + 0.5
    orders = np.arange(wanted)
    table = math.sqrt(2.0 / extent) * np.cos(math.pi * places[:, None] * orders[None, :] / extent)
    table[:, 0] *= 1.0 / math.sqrt(2.0)
    return table.astype(np.float32).astype(jnp.bfloat16).astype(np.float32)


def cycle_table(extent, half_modes):
    angles = 2.0 * math.pi * (np.arange(extent) + 0.5) / extent
    orders = np.arange(half_modes)
    cosines = math.sqrt(2.0 / extent) * np.cos(angles[:, None] * orders[None, :])
    cosines[:, 0] *= 1.0 / math.sqrt(2.0)
    sines = math.sqrt(2.0 / extent) * np.sin(angles[:, None] * (orders[None, :] + 1.0))
    table = np.concatenate([cosines, sines], axis=1)
    return table.astype(np.float32).astype(jnp.bfloat16).astype(np.float32)


def make_tables(axial, cycle, radial, cycle_devices):
    sector = cycle // cycle_devices
    pairs = 2 * MT * MR
    radial_table, axial_table = cosine_table(radial, MR), cosine_table(axial, MX)
    cycle_all = cycle_table(cycle, MT)
    tables = {}
    ends = np.zeros((32, radial), np.float32)
    ends[:MR] = radial_table.T
    ends[MR:] = 1.0
    tables["ends"] = ends
    forward = np.zeros((cycle_devices, 2 * MT, MR, 2, sector, MR), np.float32)
    for k in range(MR):
        part = cycle_all.reshape(cycle_devices, sector, 2 * MT)
        forward[:, :, k, 0, :, k] = part.transpose(0, 2, 1)
    forward = forward.reshape(cycle_devices, 2 * pairs, sector * MR)
    tables["inverse"] = forward.transpose(0, 2, 1)
    rows = np.zeros((pairs, 2, 128), np.float32)
    for p in range(pairs):
        rows[p, 1, CH if p % 8 == 7 else p // 8] = 1.0
    place = np.broadcast_to(rows.reshape(1, 2 * pairs, 128), (cycle_devices, 2 * pairs, 128))
    tables["forward"] = np.concatenate([forward, place], axis=2)
    pick = np.zeros((80, pairs, 2), np.float32)
    for i in range(CH):
        pick[i, 8 * i, 1] = 1.0
    pick[CH, 7, 1] = 1.0
    tables["pick"] = pick.reshape(80, 2 * pairs)
    gather = np.zeros((80, cycle_devices, pairs // cycle_devices, 2), np.float32)
    ax_devices = pairs // cycle_devices
    slab = axial // ax_devices
    by_slab = axial_table.reshape(ax_devices, slab, MX)
    gather[: slab * MX, :, :, 0] = by_slab.transpose(1, 2, 0).reshape(slab * MX, 1, ax_devices)
    gather[slab * MX :, :, :, 1] = 1.0
    tables["gather"] = gather.reshape(80, 2 * pairs)
    spread = np.zeros((ax_devices, 2, slab * MX), np.float32)
    spread[:, 0, :] = by_slab.reshape(ax_devices, slab * MX)
    tables["spread"] = spread.reshape(2 * ax_devices, slab * MX)
    halves = (np.arange(128)[:, None] // 64 == np.arange(128)[None, :] // 64).astype(np.float32)
    tables["halves"] = np.concatenate([halves, halves], axis=0)
    tables["radial"] = np.tile(radial_table.T, (sector, 1))
    tables["same"] = (np.arange(sector * MR)[None, :] // MR == np.arange(sector)[:, None]).astype(np.float32)
    return {name: value.astype(jnp.float32 if name == "same" else jnp.bfloat16) for name, value in tables.items()}


def gelu_slope(values):
    density = jnp.exp(-0.5 * values * values) * (1.0 / math.sqrt(2.0 * math.pi))
    return 0.5 * (1.0 + lax.erf(values * (1.0 / math.sqrt(2.0)))) + values * density


def dot_nn(a, b):
    return lax.dot_general(a, b, (((1,), (0,)), ((), ())), preferred_element_type=F32)


def dot_nt(a, b):
    return lax.dot_general(a, b, (((1,), (1,)), ((), ())), preferred_element_type=F32)


def split_halves(values):
    lane = lax.broadcasted_iota(jnp.int32, values.shape, 1)
    high = values.astype(BF).astype(F32)
    return jnp.where(lane < 64, high, pltpu.roll(values - high, 64, 1))


def first_kernel(layer_hbm, pre_hbm, grad_hbm, ends_hbm, forward_hbm,
                 slope_hbm, sent_hbm, layer, pre, grad, slope, layer_rows, grad_rows, coefs,
                 ends, forward, sent, in_sem, out_sem, table_sem, sent_sem):
    chunks, blocks = in_sem.shape[0], sent_sem.shape[0]
    group, size = CH // chunks, sent.shape[0] // blocks
    copies = []
    for c in range(chunks):
        part = pl.ds(c * group, group)
        pairs = ((pre_hbm, pre), (grad_hbm, grad), (layer_hbm, layer))
        copies.append([pltpu.make_async_copy(a.at[part], b.at[part], in_sem.at[c, n]) for n, (a, b) in enumerate(pairs)])
    pairs = ((ends_hbm, ends), (forward_hbm.at[lax.axis_index("az")], forward))
    tables = [pltpu.make_async_copy(a, b, table_sem.at[n]) for n, (a, b) in enumerate(pairs)]
    for copy in sum(copies, []) + tables:
        copy.start()
    leaving = []
    for c in range(chunks):
        part = pl.ds(c * group, group)
        copies[c][0].wait()
        copies[c][1].wait()
        slope[part] = (grad[part].astype(F32) * gelu_slope(pre[part].astype(F32))).astype(BF)
        leaving.append(pltpu.make_async_copy(slope.at[part], slope_hbm.at[part], out_sem.at[c]))
        leaving[-1].start()
        copies[c][2].wait()
        for at in range(c * group, (c + 1) * group, 16):
            for x in range(2):
                rows = slice(x * CH + at, x * CH + at + 16)
                layer_rows[:, rows, :] = jnp.swapaxes(layer[at : at + 16, x], 0, 1)
                grad_rows[:, rows, :] = jnp.swapaxes(slope[at : at + 16, x], 0, 1)
    for copy in tables:
        copy.wait()
    point = dot_nt(
        jnp.concatenate([layer_rows[t] for t in range(16)], axis=1), jnp.concatenate([grad_rows[t] for t in range(16)], axis=1)
    )
    out = dot_nt(ends[...], grad_rows[...].reshape(2048, 128))
    bias = jnp.zeros((16, 128), F32)
    for t in range(16):
        coefs[t * MR : (t + 1) * MR, :] = out[:16, t * 128 : (t + 1) * 128].astype(BF)
        bias += out[16:, t * 128 : (t + 1) * 128]
    point = point[:64] + pltpu.roll(point[64:], 64, 1)
    bias = bias + pltpu.roll(bias, 64, 1)
    sums = jnp.concatenate([split_halves(point), split_halves(bias), jnp.zeros((48, 128), F32)], axis=0).astype(BF)
    coef = jnp.concatenate([coefs[...], sums], axis=0)
    for b in range(blocks):
        rows = slice(b * size, (b + 1) * size)
        sent[rows] = dot_nn(forward[rows], coef).astype(BF)
        leaving.append(pltpu.make_async_copy(sent.at[rows], sent_hbm.at[rows], sent_sem.at[b]))
        leaving[-1].start()
    for copy in leaving:
        copy.wait()


def first(layer_input, pre_act, out_grad, tables):
    chunks, blocks = 2, 2
    shape = (CH, 2, 16, 128)
    hbm = pl.BlockSpec(memory_space=pl.ANY)
    return pl.pallas_call(
        first_kernel,
        in_specs=[hbm] * 5,
        out_specs=[hbm] * 2,
        scratch_shapes=[pltpu.VMEM(shape, BF)] * 4
        + [
            pltpu.VMEM((16, 128, 128), BF),
            pltpu.VMEM((16, 128, 128), BF),
            pltpu.VMEM((256, 128), BF),
            pltpu.VMEM((32, 128), BF),
            pltpu.VMEM((1024, 384), BF),
            pltpu.VMEM((1024, 128), BF),
            pltpu.SemaphoreType.DMA((chunks, 3)),
            pltpu.SemaphoreType.DMA((chunks,)),
            pltpu.SemaphoreType.DMA((2,)),
            pltpu.SemaphoreType.DMA((blocks,)),
        ],
        out_shape=[jax.ShapeDtypeStruct(shape, BF), jax.ShapeDtypeStruct((1024, 128), BF)],
        compiler_params=pltpu.CompilerParams(vmem_limit_bytes=60 * 1024 * 1024),
        name="slope_and_modes",
    )(layer_input, pre_act, out_grad, tables["ends"], tables["forward"])


def middle_kernel(gain, norm, got_ref, gather_ref, weight_ref, halves_ref, spread_ref, mode_ref, sent_ref, stack):
    full = dot_nn(gather_ref[...], got_ref[...])
    lane = lax.broadcasted_iota(jnp.int32, (32, 128), 1)
    picked = jnp.where(lane < 64, full[:32], full[32:64])
    mode = (gain * (picked + pltpu.roll(picked, 64, 1))).astype(BF)
    mode_ref[...] = mode
    mode_wide = mode.astype(F32)
    for c in range(32):
        product = weight_ref[0, :, c * 128 : (c + 1) * 128].astype(F32) * mode_wide
        high = product.astype(BF)
        stack[c * 32 : (c + 1) * 32, :128] = high
        stack[c * 32 : (c + 1) * 32, 128:] = (product - high.astype(F32)).astype(BF)
    chains = []
    for start in range(0, 32, 8):
        summed = dot_nn(stack[start * 32 : start * 32 + 256], halves_ref[...])
        coef = jnp.zeros((32, 128), F32)
        for c in range(8):
            coef = jnp.where(lane % 64 == start + c, summed[c * 32 : (c + 1) * 32], coef)
        chains.append(coef)
    coef = (chains[0] + chains[1]) + (chains[2] + chains[3])
    coef = jnp.concatenate([coef, pltpu.roll(coef, 32, 1)], axis=0).astype(BF)
    slabs = dot_nn(spread_ref[...], coef)
    sums = full[64:80]
    sums = split_halves((sums + pltpu.roll(sums, 64, 1)) * norm)
    row = lax.broadcasted_iota(jnp.int32, (128, 128), 0)
    slabs = jnp.where(row % 2 == 0, slabs, sums[:1]).astype(BF)
    for az in range(8):
        sent_ref[az] = slabs


def middle(got, spec_weight, tables, gain, norm):
    return pl.pallas_call(
        functools.partial(middle_kernel, gain, norm),
        out_shape=[jax.ShapeDtypeStruct((32, 128), BF), jax.ShapeDtypeStruct((8, 128, 128), BF)],
        scratch_shapes=[pltpu.VMEM((1024, 256), BF)],
        compiler_params=pltpu.CompilerParams(vmem_limit_bytes=VMEM_LIMIT),
        name="modes_and_mixing",
    )(got, tables["gather"], spec_weight, tables["halves"], tables["spread"])


def last_kernel(got_ref, pick_ref, radial_ref, same_ref, inverse_ref, point_ref,
                field_hbm, weight_hbm, bias_hbm, columns, wide, field, weight, bias, out_sem, sums_sem):
    got = got_ref[...]
    sums = dot_nn(pick_ref[...], got)
    sums = sums + pltpu.roll(sums, 64, 1)
    weight[...] = sums[:64, :64]
    bias[...] = sums[64, :64]
    leaving = [
        pltpu.make_async_copy(weight, weight_hbm, sums_sem.at[0]),
        pltpu.make_async_copy(bias, bias_hbm, sums_sem.at[1]),
    ]
    for copy in leaving:
        copy.start()
    columns[...] = jnp.transpose(dot_nn(inverse_ref[...], got))
    same = same_ref[...]
    radial = radial_ref[...]
    chunks = out_sem.shape[0]
    group = CH // chunks
    for c in range(chunks):
        for at in range(group):
            for x in range(2):
                i = c * group + at
                place = (i % 2) * 64 + x * 32 + i // 2
                value = jnp.broadcast_to(columns[place : place + 1, :], (16, 256)) * same
                wide[c, (at * 2 + x) * 16 : (at * 2 + x) * 16 + 16, :] = value.astype(BF)
        part = slice(c * group, (c + 1) * group)
        spectral = dot_nn(wide[c], radial)
        field[part] = (spectral.reshape(group, 2, 16, 128) + point_ref[part]).astype(BF)
        leaving.append(pltpu.make_async_copy(field.at[part], field_hbm.at[part], out_sem.at[c]))
        leaving[-1].start()
    for copy in leaving:
        copy.wait()


def last(got, inverse, point_part, tables):
    chunks = 4
    shape = (CH, 2, 16, 128)
    hbm, vmem = pl.BlockSpec(memory_space=pl.ANY), pl.BlockSpec(memory_space=pltpu.VMEM)
    return pl.pallas_call(
        last_kernel,
        in_specs=[vmem] * 6,
        out_specs=[hbm] * 3,
        scratch_shapes=[
            pltpu.VMEM((128, 256), F32),
            pltpu.VMEM((chunks, CH // chunks * 32, 256), BF),
            pltpu.VMEM(shape, BF),
            pltpu.VMEM((CH, CH), F32),
            pltpu.VMEM((CH,), F32),
            pltpu.SemaphoreType.DMA((chunks,)),
            pltpu.SemaphoreType.DMA((2,)),
        ],
        out_shape=[
            jax.ShapeDtypeStruct(shape, BF),
            jax.ShapeDtypeStruct((CH, CH), F32),
            jax.ShapeDtypeStruct((CH,), F32),
        ],
        compiler_params=pltpu.CompilerParams(vmem_limit_bytes=32 * 1024 * 1024),
        name="modes_to_field",
    )(got, tables["pick"], tables["radial"], tables["same"], inverse, point_part)


def exchange(rows, devices):
    sent = rows.reshape(devices, 2, 128)
    return lax.all_to_all(sent, ("az", "ax"), 0, 0, tiled=True).reshape(2 * devices, 128)


def per_device(layer_input, pre_act, out_grad, point_weight, spec_weight, saved_coeffs):
    axial_devices = lax.axis_size("ax")
    cycle_devices = lax.axis_size("az")
    devices = axial_devices * cycle_devices
    axial_total = layer_input.shape[1] * axial_devices
    cycle_total = layer_input.shape[2] * cycle_devices
    radial_length = layer_input.shape[3]
    cells_total = axial_total * cycle_total * radial_length
    gain = math.sqrt(cells_total / (2.0 * MX * MT * MR))
    norm = 1.0 / math.sqrt(cells_total)
    tables = make_tables(axial_total, cycle_total, radial_length, cycle_devices)

    grad_pre, sent = first(layer_input, pre_act, out_grad, tables)
    got = exchange(sent, devices)
    mode_grad, sent = middle(got, spec_weight, tables, gain, norm)
    got = exchange(sent.reshape(2 * devices, 128), devices)
    saved_modes = saved_coeffs.reshape(MX, CH).astype(F32)
    spec_grad = (
        (saved_modes[:, :, None] * mode_grad[:, :CH].astype(F32)[:, None, :]).astype(BF).reshape(1, MX, CH * CH)
    )
    inverse, _ = lax.optimization_barrier((tables["inverse"], mode_grad))
    inverse = lax.dynamic_index_in_dim(inverse, lax.axis_index("az"), 0, keepdims=False)
    point_part = jnp.einsum("io,oxtr->ixtr", point_weight, grad_pre, preferred_element_type=F32)
    input_grad, point_grad, bias_grad = last(got, inverse, point_part, tables)
    return (input_grad, point_grad, bias_grad, spec_grad)


def solution(mesh):
    return jax.shard_map(
        per_device,
        mesh=mesh,
        in_specs=(
            P(None, "ax", "az", None),
            P(None, "ax", "az", None),
            P(None, "ax", "az", None),
            P(),
            P(("az", "ax"), None, None),
            P(("az", "ax"), None),
        ),
        out_specs=(P(None, "ax", "az", None), P(), P(), P(("az", "ax"), None, None)),
        check_vma=False,
    )
```
